128 devices in a mesh: dp: 32 (over x, y, z_lo), mp: 4 (over z_hi, core).
Axes of the slice: x: 4, y: 4, z: 4 (z_hi: 2, z_lo: 2; z = z_hi * 2 + z_lo), core: 2. Of those that a mesh axis runs over, the one named last changes fastest.
Arguments:
- inputs: float32 [8192, 1024], P('dp'), may hold values from -6 to 6
- first_gain: float32 [1024], replicated, may hold values from 0.1 to 1.9
- first_shift: float32 [1024], replicated, may hold values from -3 to 3
- attend_weight: bfloat16 [3, 1024, 1024], P(None, None, 'mp'), may hold values from -0.25 to 0.25
- attend_bias: float32 [2, 1024], P(None, 'mp'), may hold values from -3 to 3
- output_weight: bfloat16 [1024, 1024], P('mp'), may hold values from -1 to 1
- output_bias: float32 [1024], replicated, may hold values from -3 to 3
- second_gain: float32 [1024], replicated, may hold values from 0.1 to 1.9
- second_shift: float32 [1024], replicated, may hold values from -3 to 3
- up_weight: bfloat16 [1024, 4096], P(None, 'mp'), may hold values from -0.1875 to 0.1875
- up_bias: float32 [4096], P('mp'), may hold values from -3 to 3
- down_weight: bfloat16 [4096, 1024], P('mp'), may hold values from -0.125 to 0.125
- down_bias: float32 [1024], replicated, may hold values from -3 to 3
- image_of: int32 [32], replicated, may hold values from 0 to 2, as said below
- cotangent: float32 [8192, 1024], P('dp'), may hold values from -6 to 6
Outputs:
- result: float32 [8192, 1024], P('dp')
- input_grad: float32 [8192, 1024], P('dp')
- first_gain_grad: float32 [1024], replicated
- first_shift_grad: float32 [1024], replicated
- attend_weight_grad: float32 [3, 1024, 1024], P(None, None, 'mp')
- attend_bias_grad: float32 [2, 1024], P(None, 'mp')
- output_weight_grad: float32 [1024, 1024], P('mp')
- output_bias_grad: float32 [1024], replicated
- second_gain_grad: float32 [1024], replicated
- second_shift_grad: float32 [1024], replicated
- up_weight_grad: float32 [1024, 4096], P(None, 'mp')
- up_bias_grad: float32 [4096], P('mp')
- down_weight_grad: float32 [4096, 1024], P('mp')
- down_bias_grad: float32 [1024], replicated
The draws below stay inside these ranges and needn't reach their ends.
Inputs may be any that keep to these rules, and one draw needn't show every extreme that they name: `image_of`: three images: one holds the patches of 16 indices of dp, among them the first and the last index; the other two hold 8 indices each; which image is which is drawn.
All inputs are finite; a program needn't handle non-finite values.
Results may differ from the reference program's by a relative error of at most 0.035.
Values may be sent and summed in bfloat16 or wider, within the bound.
A program may use at most 128 MiB of HBM per device.

```python
import jax
import jax.numpy as jnp
from jax import lax

D = 1024
HEADS = 16
FF = 4096
HEAD_DIM = 64
TOK = 256
TOTAL = 8192
N_DP = 32


def draw_image_of(key, part):
    key = jax.random.fold_in(key, 11)
    first_key, second_key = jax.random.split(key)
    inner = (jax.random.permutation(first_key, N_DP - 2) + 1).astype(jnp.int32)
    order = jnp.concatenate([jnp.array([0, N_DP - 1], jnp.int32), inner])
    ranked = jnp.arange(N_DP, dtype=jnp.int32)
    classes = jnp.where(ranked < N_DP // 2, 0, jnp.where(ranked < 3 * N_DP // 4, 1, 2))
    labels = jax.random.permutation(second_key, 3).astype(jnp.int32)
    return jnp.zeros((N_DP,), jnp.int32).at[order].set(labels[classes])


def steps_of(stream_key, dims, pieces, low, high):
    level, own = 1.0, jax.random.fold_in(stream_key, 6)
    for position, shards_of in pieces:
        draws = jnp.exp(jax.random.uniform(jax.random.fold_in(own, position), (shards_of,), jnp.float32, low / len(pieces), high / len(pieces)))
        level = level * jnp.repeat(draws, dims[position] // shards_of).reshape([-1 if axis == position else 1 for axis in range(len(dims))])
    return level


def normal_values(key, extent, deviation, bound, cuts=(), held_as=jnp.bfloat16):
    gain = steps_of(key, extent, cuts, -0.22, 0.18) if cuts else 1.0
    values = jax.random.normal(key, extent, jnp.float32) * deviation * gain
    return jnp.minimum(jnp.maximum(values, -bound), bound).astype(held_as)


def setup_inputs(seed: int = 0) -> dict:
    key_of = jax.random.split(jax.random.key(seed), 16)
    inputs = normal_values(key_of[0], (TOTAL, D), 1.0, 6.0, ((0, 32),), jnp.float32)
    first_gain = jnp.clip(1.0 + 0.18 * jax.random.normal(key_of[1], (D,), jnp.float32), 0.1, 1.9)
    first_shift = normal_values(key_of[2], (D,), 0.5, 3.0, (), jnp.float32)
    attend_weight = normal_values(key_of[3], (3, D, D), (D // 2) ** -0.5, 0.25, ((2, 4),))
    attend_bias = normal_values(key_of[4], (2, D), 0.5, 3.0, ((1, 4),), jnp.float32)
    output_weight = normal_values(key_of[5], (D, D), (D // 32) ** -0.5, 1.0, ((0, 4),))
    output_bias = normal_values(key_of[6], (D,), 0.5, 3.0, (), jnp.float32)
    second_gain = jnp.clip(1.0 + 0.18 * jax.random.normal(key_of[7], (D,), jnp.float32), 0.1, 1.9)
    second_shift = normal_values(key_of[8], (D,), 0.5, 3.0, (), jnp.float32)
    up_weight = normal_values(key_of[9], (D, FF), D ** -0.5, 0.1875, ((1, 4),))
    up_bias = normal_values(key_of[10], (FF,), 0.5, 3.0, ((0, 4),), jnp.float32)
    down_weight = normal_values(key_of[11], (FF, D), (FF // 2) ** -0.5, 0.125, ((0, 4),))
    down_bias = normal_values(key_of[12], (D,), 0.5, 3.0, (), jnp.float32)
    image_of = draw_image_of(jax.random.fold_in(key_of[15], 71), 0)
    cotangent = normal_values(key_of[14], (TOTAL, D), 1.0, 6.0, ((0, 32),), jnp.float32)
    return dict(inputs=inputs, first_gain=first_gain, first_shift=first_shift, attend_weight=attend_weight, attend_bias=attend_bias, output_weight=output_weight, output_bias=output_bias, second_gain=second_gain, second_shift=second_shift, up_weight=up_weight, up_bias=up_bias, down_weight=down_weight, down_bias=down_bias, image_of=image_of, cotangent=cotangent)


@jax.custom_vjp
def low(v):
    return lax.optimization_barrier(v.astype(jnp.bfloat16)).astype(jnp.float32)

@jax.custom_vjp
def low_back(v):
    return v

def low_keep(v):
    return (low(v), None)

def low_pass(kept, grad):
    return (grad,)

def back_keep(v):
    return (v, None)

def back_low(kept, grad):
    return (low(grad),)
low.defvjp(low_keep, low_pass)
low_back.defvjp(back_keep, back_low)
EPSILON = 1e-06

def layer_norm(values, norm_gain, norm_shift):
    row_mean = lax.optimization_barrier(jnp.mean(values, axis=-1, keepdims=True))
    centred = values - row_mean
    variance = lax.optimization_barrier(jnp.mean(centred * centred, axis=-1, keepdims=True))
    return centred * lax.rsqrt(variance + EPSILON) * norm_gain + norm_shift

def gelu_exact(values):
    return jax.nn.gelu(values, approximate=False)

def matmul(left, right):
    return jnp.dot(left, right, precision=lax.Precision.HIGHEST)

def reference(inputs, first_gain, first_shift, attend_weight, attend_bias, output_weight, output_bias, second_gain, second_shift, up_weight, up_bias, down_weight, down_bias, image_of, cotangent):
    token_image = jnp.repeat(image_of, TOK)
    query_rows = min(256, TOTAL)
    factor = HEAD_DIM ** (-0.5)

    def forward(inputs, first_gain, first_shift, attend_weight, attend_bias, output_weight, output_bias, second_gain, second_shift, up_weight, up_bias, down_weight, down_bias):
        first_low = low(layer_norm(inputs, first_gain, first_shift))
        queries = low(low_back(matmul(first_low, attend_weight[0]) + attend_bias[0]))
        keys_full = low(low_back(matmul(first_low, attend_weight[1])))
        values_full = low(low_back(matmul(first_low, attend_weight[2]) + attend_bias[1]))
        key_heads = keys_full.reshape(TOTAL, HEADS, HEAD_DIM)
        value_heads = values_full.reshape(TOTAL, HEADS, HEAD_DIM)
        query_blocks = queries.reshape(TOTAL // query_rows, query_rows, HEADS, HEAD_DIM)
        image_blocks = token_image.reshape(TOTAL // query_rows, query_rows)

        def attend(block_item):
            query_blk, image_blk = block_item
            scores = jnp.einsum('qhd,khd->hqk', query_blk, key_heads, precision=lax.Precision.HIGHEST) * factor
            scores = low_back(scores)
            allowed = (image_blk[:, None] == token_image[None, :])[None]
            scores = jnp.where(allowed, scores, -1e+30)
            probs = low(jax.nn.softmax(scores, axis=-1))
            return jnp.einsum('hqk,khd->qhd', probs, value_heads, precision=lax.Precision.HIGHEST)
        attended = lax.map(jax.checkpoint(attend), (query_blocks, image_blocks)).reshape(TOTAL, D)
        attended = low(low_back(attended))
        hidden = inputs + low_back(matmul(attended, output_weight) + output_bias)
        second_low = low(layer_norm(hidden, second_gain, second_shift))
        activated = low(gelu_exact(low_back(matmul(second_low, up_weight) + up_bias)))
        return hidden + low_back(matmul(activated, down_weight) + down_bias)
    result, back_fn = jax.vjp(forward, inputs, first_gain, first_shift, attend_weight.astype(jnp.float32), attend_bias, output_weight.astype(jnp.float32), output_bias, second_gain, second_shift, up_weight.astype(jnp.float32), up_bias, down_weight.astype(jnp.float32), down_bias)
    grads = back_fn(cotangent)
    return (result, grads[0], grads[1], grads[2], grads[3], grads[4], grads[5], grads[6], grads[7], grads[8], grads[9], grads[10], grads[11], grads[12])
```

```python
import functools

import jax
import jax.numpy as jnp
from jax import lax
from jax.experimental import pallas as pl
from jax.experimental.pallas import tpu as pltpu
from jax.sharding import PartitionSpec as P

HEAD_DIM = 64
EPSILON = 1e-06
LOWEST = -1e30
HIGHEST = 1e30
MESH = pl.DeviceIdType.MESH
F32 = jnp.float32
BF16 = jnp.bfloat16
VMEM_BYTES = 60 * 2**20


def dot_nn(left, right):
    return lax.dot_general(left, right, (((1,), (0,)), ((), ())), preferred_element_type=F32)


def dot_nt(left, right):
    return lax.dot_general(left, right, (((1,), (1,)), ((), ())), preferred_element_type=F32)


def dot_tn(left, right):
    return lax.dot_general(left, right, (((0,), (0,)), ((), ())), preferred_element_type=F32)


class Place:
    def __init__(self):
        data, model = lax.axis_index("dp"), lax.axis_index("mp")
        self.x = lax.div(data, 8)
        self.y = lax.rem(lax.div(data, 2), 4)
        self.z = lax.rem(data, 2)
        self.high = lax.div(model, 2)
        self.core = lax.rem(model, 2)
        self.group = self.y * 2 + self.z

    def at(self, dx=0, dy=0, dz=0, dhigh=0, dcore=0):
        x = lax.rem(self.x + dx, 4)
        y = lax.rem(self.y + dy, 4)
        z = lax.rem(self.z + dz, 2)
        high = lax.rem(self.high + dhigh, 2)
        core = lax.rem(self.core + dcore, 2)
        return (x * 8 + y * 2 + z, high * 2 + core)


class Links:
    def __init__(self, send_sem, recv_sem):
        self.send_sem, self.recv_sem = send_sem, recv_sem
        self.used = 0
        self.sent = []

    def copy(self, source, target, device):
        at = self.used
        self.used += 1
        made = pltpu.make_async_remote_copy(
            src_ref=source,
            dst_ref=target,
            send_sem=self.send_sem.at[at],
            recv_sem=self.recv_sem.at[at],
            device_id=device,
            device_id_type=MESH,
        )
        self.sent.append(made)
        return made

    def send(self, source, target, device):
        made = self.copy(source, target, device)
        made.start()
        return made

    def finish(self):
        for made in self.sent:
            made.wait_send()
        self.sent = []


def greet(partners):
    barrier = pltpu.get_barrier_semaphore()
    for device in partners:
        pl.semaphore_signal(barrier, inc=1, device_id=device, device_id_type=MESH)
    return lambda: pl.semaphore_wait(barrier, len(partners))


def all_partners(me):
    return [
        me.at(dx=1), me.at(dx=3), me.at(dx=2), me.at(dy=1), me.at(dy=3),
        me.at(dz=1), me.at(dhigh=1), me.at(dcore=1),
    ]


def row_norm(values):
    mean = jnp.mean(values, axis=-1, keepdims=True)
    centred = values - mean
    variance = jnp.mean(centred * centred, axis=-1, keepdims=True)
    inverse = lax.rsqrt(variance + EPSILON)
    return centred * inverse, inverse


def spread(column):
    return jnp.broadcast_to(column, (column.shape[0], 128))


class Gather:
    def __init__(self, me, links, slots, rows):
        self.me, self.links, self.slots = me, links, slots
        self.low = pl.ds(0, rows // 2)
        self.high = pl.ds(rows // 2, rows // 2)
        self.other = 1 - me.z

    def slot(self, dy, z):
        return lax.rem(self.me.y + dy, 4) * 2 + z

    def send(self, slot, device):
        return self.links.send(self.slots.at[slot], self.slots.at[slot], device)

    def begin(self):
        me = self.me
        own = me.group
        self.from_z = self.send(own, me.at(dz=1))
        self.own_y = [self.send(own, me.at(dy=1)), self.send(own, me.at(dy=3))]

    def pass_z(self):
        me = self.me
        self.from_z.wait_recv()
        slot = self.slot(0, self.other)
        self.other_y = [self.send(slot, me.at(dy=1)), self.send(slot, me.at(dy=3))]

    def forward(self, pair, z):
        me = self.me
        pair[0].wait_recv()
        below = self.slot(3, z)
        up = self.links.send(
            self.slots.at[below, self.low], self.slots.at[below, self.low], me.at(dy=1)
        )
        pair[1].wait_recv()
        above = self.slot(1, z)
        down = self.links.send(
            self.slots.at[above, self.high], self.slots.at[above, self.high], me.at(dy=3)
        )
        return [up, down]

    def pass_own(self):
        self.far_own = self.forward(self.own_y, self.me.z)

    def pass_other(self):
        self.far_other = self.forward(self.other_y, self.other)

    def end_own(self):
        for made in self.far_own:
            made.wait_recv()

    def end_other(self):
        for made in self.far_other:
            made.wait_recv()


def attention_kernel(
    x_ref, gain_ref, shift_ref, weight_ref, bias_ref, output_ref, image_ref,
    first_out, kv_out, query_out, mixed_out, stats_out, attended_out, output_out,
    kv, query_pair, kv_send, query_send, query_own, top, total, mixed,
    head_send, head_recv, attended, output_all, send_sem, recv_sem,
):
    me = Place()
    links = Links(send_sem, recv_sem)
    wait_all = greet(all_partners(me))

    normed, _ = row_norm(x_ref[...])
    first_low = (normed * gain_ref[...] + shift_ref[...]).astype(BF16)
    first_out[...] = first_low
    keys = dot_nn(first_low, weight_ref[1])
    values = dot_nn(first_low, weight_ref[2]) + bias_ref[1:2, :]
    for head in range(4):
        part = slice(head * HEAD_DIM, (head + 1) * HEAD_DIM)
        kv_send[head] = jnp.concatenate([keys[:, part], values[:, part]], axis=1).astype(BF16)
    queries = dot_nn(first_low, weight_ref[0]) + bias_ref[0:1, :]
    queries = queries.astype(BF16).astype(F32) * (HEAD_DIM**-0.5)
    for head in range(4):
        part = slice(head * HEAD_DIM, (head + 1) * HEAD_DIM)
        query_send[head] = jnp.concatenate(
            [queries[:128, part], queries[128:, part]], axis=1
        ).astype(BF16)

    wait_all()
    own = me.group
    kv_moves, query_moves = [], []
    for step in (1, 3, 2):
        head = lax.rem(me.x + step, 4)
        kv_moves.append(
            links.send(kv_send.at[head], kv.at[own, pl.ds(me.x * 256, 256)], me.at(dx=step))
        )
    for step in (1, 3, 2):
        head = lax.rem(me.x + step, 4)
        query_moves.append(
            links.send(
                query_send.at[head], query_pair.at[own, pl.ds(me.x * 128, 128)], me.at(dx=step)
            )
        )
    kv[own, pl.ds(me.x * 256, 256), :] = kv_send[me.x]
    query_pair[own, pl.ds(me.x * 128, 128), :] = query_send[me.x]
    attended_at = me.high * 2 + me.core

    for made in kv_moves:
        made.wait_recv()
    gather = Gather(me, links, kv, 1024)
    gather.begin()
    output_all[attended_at] = output_ref[...]
    output_high = links.send(output_ref, output_all.at[attended_at], me.at(dhigh=1))
    output_core = links.send(output_ref, output_all.at[attended_at], me.at(dcore=1))
    for made in query_moves:
        made.wait_recv()
    for block in range(4):
        pair = query_pair[own, block * 128 : (block + 1) * 128, :].astype(F32)
        both = jnp.concatenate([pair, pltpu.roll(pair, 64, 1)], axis=0)
        lane = lax.broadcasted_iota(jnp.int32, both.shape, 1)
        query_own[block * 256 : (block + 1) * 256, :] = jnp.where(
            lane < HEAD_DIM, both, 0.0
        ).astype(BF16)
    query_gather = Gather(me, links, query_pair, 512)
    top[...] = jnp.full(top.shape, LOWEST, F32)
    total[...] = jnp.zeros(total.shape, F32)
    mixed[...] = jnp.zeros(mixed.shape, F32)

    def attend(slot):
        @pl.loop(0, 4)
        def _(block):
            rows = pl.ds(pl.multiple_of(block * 256, 256), 256)
            query = query_own[rows, :]
            mine = image_ref[block * 8 + own]
            scores, shut = [], []
            highest = None
            for part in range(4):
                same = image_ref[part * 8 + slot] == mine
                shut.append(jnp.where(same, -3e38, HIGHEST))
                score = dot_nt(query, kv[slot, part * 256 : (part + 1) * 256, :])
                scores.append(score)
                peak = jnp.maximum(score[:, :128], score[:, 128:])
                peak = jnp.minimum(peak, jnp.where(same, 3e38, LOWEST))
                highest = peak if highest is None else jnp.maximum(highest, peak)
            before = top[rows, :]
            now = jnp.maximum(before, spread(jnp.max(highest, axis=1, keepdims=True)))
            fade = jnp.exp(before - now)
            top[rows, :] = now
            sums = total[rows, :] * fade
            acc = mixed[rows, :] * fade
            for part in range(4):
                level = jnp.maximum(now, shut[part])
                prob = jnp.exp(scores[part] - jnp.concatenate([level, level], axis=1))
                sums = sums + prob[:, :128] + prob[:, 128:]
                acc = acc + dot_nn(prob.astype(BF16), kv[slot, part * 256 : (part + 1) * 256, :])
            total[rows, :] = sums
            mixed[rows, :] = acc

    attend(own)
    gather.pass_z()
    attend(gather.slot(0, gather.other))
    gather.pass_own()
    query_gather.begin()
    attend(gather.slot(3, me.z))
    attend(gather.slot(1, me.z))
    gather.pass_other()
    query_gather.pass_z()
    attend(gather.slot(3, gather.other))
    attend(gather.slot(1, gather.other))
    output_high.wait_recv()
    across = lax.rem(me.high + 1, 2) * 2 + me.core
    output_pass = links.send(output_all.at[across], output_all.at[across], me.at(dcore=1))
    gather.end_own()
    attend(gather.slot(2, me.z))
    gather.end_other()
    attend(gather.slot(2, gather.other))

    for block in range(4):
        rows = slice(block * 256, (block + 1) * 256)
        sums = spread(jnp.sum(total[rows, :], axis=1, keepdims=True))
        out = mixed[rows, :] / sums
        mixed[rows, :] = out
        log_total = top[rows, :] + jnp.log(sums)
        stats_out[block : block + 1, :] = log_total.T[0:1, :]
        back = pltpu.roll(out[:128, :], 64, 1)
        lane = lax.broadcasted_iota(jnp.int32, back.shape, 1)
        head_send[block] = jnp.where(lane < HEAD_DIM, back, out[128:, :]).astype(BF16)
    stats_out[4:, :] = jnp.zeros((4, 256), F32)
    head_moves = []
    for step in (1, 3, 2):
        to = lax.rem(me.x + step, 4)
        head_moves.append(links.send(head_send.at[to], head_recv.at[me.x], me.at(dx=step)))
    head_recv[me.x] = head_send[me.x]
    query_gather.pass_own()
    for made in head_moves:
        made.wait_recv()
    upper = jnp.concatenate([head_recv[head].astype(F32)[:, :64] for head in range(4)], axis=1)
    lower = jnp.concatenate([head_recv[head].astype(F32)[:, 64:] for head in range(4)], axis=1)
    attended[attended_at] = jnp.concatenate([upper, lower], axis=0).astype(BF16)
    here = attended.at[attended_at]
    attended_high = links.send(here, here, me.at(dhigh=1))
    attended_core = links.send(here, here, me.at(dcore=1))
    query_gather.pass_other()
    mixed_out[...] = mixed[...]
    kv_out[...] = kv[...]
    output_core.wait_recv()
    output_pass.wait_recv()
    output_out[...] = output_all[...]
    attended_high.wait_recv()
    attended_pass = links.send(attended.at[across], attended.at[across], me.at(dcore=1))
    query_gather.end_own()
    query_gather.end_other()
    query_out[...] = query_pair[...]
    attended_core.wait_recv()
    attended_pass.wait_recv()
    attended_out[...] = attended[...]
    links.finish()


def attention(x, gain, shift, weight, bias, output_weight, image_of):
    vmem = pl.BlockSpec(memory_space=pltpu.VMEM)
    return pl.pallas_call(
        attention_kernel,
        out_shape=[
            jax.ShapeDtypeStruct((256, 1024), BF16),
            jax.ShapeDtypeStruct((8, 1024, 128), BF16),
            jax.ShapeDtypeStruct((8, 512, 128), BF16),
            jax.ShapeDtypeStruct((1024, 128), F32),
            jax.ShapeDtypeStruct((8, 256), F32),
            jax.ShapeDtypeStruct((4, 256, 256), BF16),
            jax.ShapeDtypeStruct((4, 256, 1024), BF16),
        ],
        in_specs=[vmem] * 6 + [pl.BlockSpec(memory_space=pltpu.SMEM)],
        out_specs=[vmem] * 7,
        scratch_shapes=[
            pltpu.VMEM((8, 1024, 128), BF16),
            pltpu.VMEM((8, 512, 128), BF16),
            pltpu.VMEM((4, 256, 128), BF16),
            pltpu.VMEM((4, 128, 128), BF16),
            pltpu.VMEM((1024, 128), BF16),
            pltpu.VMEM((1024, 128), F32),
            pltpu.VMEM((1024, 128), F32),
            pltpu.VMEM((1024, 128), F32),
            pltpu.VMEM((4, 128, 128), BF16),
            pltpu.VMEM((4, 128, 128), BF16),
            pltpu.VMEM((4, 256, 256), BF16),
            pltpu.VMEM((4, 256, 1024), BF16),
            pltpu.SemaphoreType.DMA((40,)),
            pltpu.SemaphoreType.DMA((40,)),
        ],
        compiler_params=pltpu.CompilerParams(
            collective_id=0, has_side_effects=True, vmem_limit_bytes=VMEM_BYTES
        ),
    )(x, gain, shift, weight, bias, output_weight, image_of)


def layer_norm(values, norm_gain, norm_shift):
    row_mean = jnp.mean(values, axis=-1, keepdims=True)
    centred = values - row_mean
    variance = jnp.mean(centred * centred, axis=-1, keepdims=True)
    return centred * lax.rsqrt(variance + EPSILON) * norm_gain + norm_shift


def gelu_exact(values):
    return jax.nn.gelu(values, approximate=False)


def block_split(pieces, row_count):
    per_block = 1
    while pieces % (per_block * 2) == 0 and per_block * 2 * row_count <= 1024:
        per_block = per_block * 2
    return pieces // per_block


def contract_rows(left, right):
    return lax.dot_general(
        left, right, (((0,), (0,)), ((), ())), preferred_element_type=jnp.float32
    )


def contract_cols(left, right):
    return lax.dot_general(
        left, right, (((1,), (1,)), ((), ())), preferred_element_type=jnp.float32
    )


def per_device(
    inputs,
    first_gain,
    first_shift,
    attend_weight,
    attend_bias,
    output_weight,
    output_bias,
    second_gain,
    second_shift,
    up_weight,
    up_bias,
    down_weight,
    down_bias,
    image_of,
    cotangent,
):
    row_count = inputs.shape[0]
    local_width = attend_weight.shape[2]
    heads_here = local_width // HEAD_DIM
    factor = HEAD_DIM ** (-0.5)
    device_count = lax.axis_size("dp")
    own_image = image_of[lax.axis_index("dp")]
    blocks = block_split(device_count, row_count)
    key_image = jnp.repeat(image_of, row_count).reshape(blocks, -1)

    def touches(image_blk):
        return jnp.any(image_blk == own_image)

    normed_one, first_back = jax.vjp(layer_norm, inputs, first_gain, first_shift)
    first_low = normed_one.astype(jnp.bfloat16)
    projected = jnp.einsum(
        "td,cdf->ctf", first_low, attend_weight, preferred_element_type=jnp.float32
    )
    queries = (projected[0] + attend_bias[0]).astype(jnp.bfloat16)
    keys_low = projected[1].astype(jnp.bfloat16)
    values_low = (projected[2] + attend_bias[1]).astype(jnp.bfloat16)
    gathered = (
        lax.all_gather(keys_low, "dp", axis=0, tiled=True),
        lax.all_gather(values_low, "dp", axis=0, tiled=True),
    )

    def as_blocks(gathered_rows):
        return gathered_rows.reshape(blocks, -1, heads_here, HEAD_DIM)

    key_blocks = as_blocks(gathered[0])
    value_blocks = as_blocks(gathered[1])
    query_heads = queries.reshape(row_count, heads_here, HEAD_DIM)

    def masked_scores(keys_blk, image_blk):
        scores = (
            jnp.einsum("qhd,khd->hqk", query_heads, keys_blk, preferred_element_type=jnp.float32)
            * factor
        )
        allowed = (image_blk == own_image)[None, None, :]
        return (jnp.where(allowed, scores, -1e30), allowed)

    def stats_step(state_pair, block_item):

        def stats_work(pair):
            running_max, running_sum = pair
            scores, allowed = masked_scores(block_item[0], block_item[1])
            new_max = jnp.maximum(running_max, jnp.max(scores, axis=2))
            shifted = jnp.where(allowed, jnp.exp(scores - new_max[:, :, None]), 0.0)
            return (
                new_max,
                running_sum * jnp.exp(running_max - new_max) + jnp.sum(shifted, axis=2),
            )

        return (lax.cond(touches(block_item[1]), stats_work, lambda pair: pair, state_pair), None)

    start_max = jnp.full((heads_here, row_count), -1e30, jnp.float32)
    (final_max, final_sum), unused = lax.scan(
        stats_step, (start_max, jnp.zeros_like(start_max)), (key_blocks, key_image)
    )
    log_total = final_max + jnp.log(final_sum)

    def block_probs(keys_blk, image_blk):
        scores, allowed = masked_scores(keys_blk, image_blk)
        return jnp.where(allowed, jnp.exp(scores - log_total[:, :, None]), 0.0)

    def value_step(summed, block_item):

        def value_work(total):
            probs = block_probs(block_item[0], block_item[2])
            return total + jnp.einsum(
                "hqk,khd->qhd",
                probs.astype(jnp.bfloat16),
                block_item[1],
                preferred_element_type=jnp.float32,
            )

        return (lax.cond(touches(block_item[2]), value_work, lambda total: total, summed), None)

    attended, unused = lax.scan(
        value_step,
        jnp.zeros((row_count, heads_here, HEAD_DIM), jnp.float32),
        (key_blocks, value_blocks, key_image),
    )
    attended = attended.reshape(row_count, local_width)
    attended_low = attended.astype(jnp.bfloat16)
    _, _, _, _, _, attended_all, output_all = attention(
        inputs, first_gain[None], first_shift[None], attend_weight, attend_bias, output_weight, image_of
    )
    hidden = (
        inputs
        + jnp.einsum("stf,sfd->td", attended_all, output_all, preferred_element_type=jnp.float32)
        + output_bias
    )
    normed_two, second_back = jax.vjp(layer_norm, hidden, second_gain, second_shift)
    second_low = normed_two.astype(jnp.bfloat16)
    pre_act = jnp.dot(second_low, up_weight, preferred_element_type=jnp.float32) + up_bias
    activated, gelu_back = jax.vjp(gelu_exact, pre_act)
    activated_low = activated.astype(jnp.bfloat16)
    unit_total = lax.psum(
        jnp.dot(activated_low, down_weight, preferred_element_type=jnp.float32).astype(
            jnp.bfloat16
        ),
        "mp",
    ).astype(jnp.float32)
    result = hidden + unit_total + down_bias
    down_grad = cotangent.astype(jnp.bfloat16)
    down_bias_grad = jnp.sum(down_grad.astype(jnp.float32), axis=0)
    down_weight_grad = contract_rows(activated_low, down_grad)
    (pre_grad,) = gelu_back(contract_cols(down_grad, down_weight))
    pre_low = pre_grad.astype(jnp.bfloat16)
    up_bias_grad = jnp.sum(pre_low.astype(jnp.float32), axis=0)
    up_weight_grad = contract_rows(second_low, pre_low)
    second_norm_grad = lax.psum(
        contract_cols(pre_low, up_weight).astype(jnp.bfloat16), "mp"
    ).astype(jnp.float32)
    hidden_part, second_gain_grad, second_shift_grad = second_back(second_norm_grad)
    hidden_grad = cotangent + hidden_part
    branch_low = hidden_grad.astype(jnp.bfloat16)
    output_bias_grad = jnp.sum(branch_low.astype(jnp.float32), axis=0)
    output_weight_grad = contract_rows(attended_low, branch_low)
    attended_grad = contract_cols(branch_low, output_weight).astype(jnp.bfloat16)
    grad_heads = attended_grad.reshape(row_count, heads_here, HEAD_DIM)
    row_delta = jnp.einsum(
        "qhd,qhd->hq",
        grad_heads.astype(jnp.float32),
        attended.reshape(row_count, heads_here, HEAD_DIM),
    )
    fresh = lax.optimization_barrier((keys_low, values_low, attended_grad))
    again = (
        lax.all_gather(fresh[0], "dp", axis=0, tiled=True),
        lax.all_gather(fresh[1], "dp", axis=0, tiled=True),
    )
    back_keys = as_blocks(again[0])
    back_values = as_blocks(again[1])

    def score_grads(keys_blk, values_blk, image_blk):
        probs = block_probs(keys_blk, image_blk)
        prob_grad = jnp.einsum(
            "qhd,khd->hqk", grad_heads, values_blk, preferred_element_type=jnp.float32
        )
        return (probs, (probs * (prob_grad - row_delta[:, :, None])).astype(jnp.bfloat16))

    zero_rows = jnp.zeros((row_count, heads_here, HEAD_DIM), jnp.float32)

    def grad_step(summed, block_item):
        keys_blk, values_blk, image_blk = block_item
        empty_part = jnp.zeros(keys_blk.shape, jnp.float32)

        def grad_work(total):
            probs, score_grad = score_grads(keys_blk, values_blk, image_blk)
            total = total + jnp.einsum(
                "hqk,khd->qhd", score_grad, keys_blk, preferred_element_type=jnp.float32
            )
            key_part = (
                jnp.einsum(
                    "hqk,qhd->khd", score_grad, query_heads, preferred_element_type=jnp.float32
                )
                * factor
            )
            value_part = jnp.einsum(
                "hqk,qhd->khd",
                probs.astype(jnp.bfloat16),
                grad_heads,
                preferred_element_type=jnp.float32,
            )
            return (total, (key_part, value_part))

        return lax.cond(
            touches(image_blk), grad_work, lambda total: (total, (empty_part, empty_part)), summed
        )

    query_sum, (key_terms, value_terms) = lax.scan(
        grad_step, zero_rows, (back_keys, back_values, key_image)
    )
    key_terms = key_terms.reshape(-1, local_width)
    value_terms = value_terms.reshape(-1, local_width)
    key_share, value_share = (
        lax.psum_scatter(
            key_terms.astype(jnp.bfloat16), "dp", scatter_dimension=0, tiled=True
        ).astype(jnp.float32),
        lax.psum_scatter(
            value_terms.astype(jnp.bfloat16), "dp", scatter_dimension=0, tiled=True
        ).astype(jnp.float32),
    )
    query_low = (query_sum.reshape(row_count, local_width) * factor).astype(jnp.bfloat16)
    key_low_grad = key_share.astype(jnp.bfloat16)
    value_low_grad = value_share.astype(jnp.bfloat16)
    stacked = jnp.stack([query_low, key_low_grad, value_low_grad])
    attend_weight_grad = jnp.einsum(
        "td,ctf->cdf", first_low, stacked, preferred_element_type=jnp.float32
    )
    attend_bias_grad = jnp.stack(
        [
            jnp.sum(query_low.astype(jnp.float32), axis=0),
            jnp.sum(value_low_grad.astype(jnp.float32), axis=0),
        ]
    )
    first_norm_grad = lax.psum(
        jnp.einsum(
            "ctf,cdf->td", stacked, attend_weight, preferred_element_type=jnp.float32
        ).astype(jnp.bfloat16),
        "mp",
    ).astype(jnp.float32)
    input_part, first_gain_grad, first_shift_grad = first_back(first_norm_grad)
    input_grad = hidden_grad + input_part
    summed_grads = (
        lax.psum(first_gain_grad.astype(jnp.bfloat16), "dp").astype(jnp.float32),
        lax.psum(first_shift_grad.astype(jnp.bfloat16), "dp").astype(jnp.float32),
        lax.psum(attend_weight_grad.astype(jnp.bfloat16), "dp").astype(jnp.float32),
        lax.psum(attend_bias_grad.astype(jnp.bfloat16), "dp").astype(jnp.float32),
        lax.psum(output_weight_grad.astype(jnp.bfloat16), "dp").astype(jnp.float32),
        lax.psum(output_bias_grad.astype(jnp.bfloat16), "dp").astype(jnp.float32),
        lax.psum(second_gain_grad.astype(jnp.bfloat16), "dp").astype(jnp.float32),
        lax.psum(second_shift_grad.astype(jnp.bfloat16), "dp").astype(jnp.float32),
        lax.psum(up_weight_grad.astype(jnp.bfloat16), "dp").astype(jnp.float32),
        lax.psum(up_bias_grad.astype(jnp.bfloat16), "dp").astype(jnp.float32),
        lax.psum(down_weight_grad.astype(jnp.bfloat16), "dp").astype(jnp.float32),
        lax.psum(down_bias_grad.astype(jnp.bfloat16), "dp").astype(jnp.float32),
    )
    return (
        result,
        input_grad,
        summed_grads[0],
        summed_grads[1],
        summed_grads[2],
        summed_grads[3],
        summed_grads[4],
        summed_grads[5],
        summed_grads[6],
        summed_grads[7],
        summed_grads[8],
        summed_grads[9],
        summed_grads[10],
        summed_grads[11],
    )


def solution(mesh):
    in_specs = (
        P("dp", None),
        P(),
        P(),
        P(None, None, "mp"),
        P(None, "mp"),
        P("mp", None),
        P(),
        P(),
        P(),
        P(None, "mp"),
        P("mp"),
        P("mp", None),
        P(),
        P(),
        P("dp", None),
    )
    out_specs = (
        P("dp", None),
        P("dp", None),
        P(),
        P(),
        P(None, None, "mp"),
        P(None, "mp"),
        P("mp", None),
        P(),
        P(),
        P(),
        P(None, "mp"),
        P("mp"),
        P("mp", None),
        P(),
    )
    return jax.shard_map(
        per_device, mesh=mesh, in_specs=in_specs, out_specs=out_specs, check_vma=False
    )
```

```python
import functools

import jax
import jax.numpy as jnp
from jax import lax
from jax.experimental import pallas as pl
from jax.experimental.pallas import tpu as pltpu
from jax.sharding import PartitionSpec as P

HEAD_DIM = 64
EPSILON = 1e-06
LOWEST = -1e30
HIGHEST = 1e30
MESH = pl.DeviceIdType.MESH
F32 = jnp.float32
BF16 = jnp.bfloat16
VMEM_BYTES = 60 * 2**20


def dot_nn(left, right):
    return lax.dot_general(left, right, (((1,), (0,)), ((), ())), preferred_element_type=F32)


def dot_nt(left, right):
    return lax.dot_general(left, right, (((1,), (1,)), ((), ())), preferred_element_type=F32)


def dot_tn(left, right):
    return lax.dot_general(left, right, (((0,), (0,)), ((), ())), preferred_element_type=F32)


class Place:
    def __init__(self):
        data, model = lax.axis_index("dp"), lax.axis_index("mp")
        self.x = lax.div(data, 8)
        self.y = lax.rem(lax.div(data, 2), 4)
        self.z = lax.rem(data, 2)
        self.high = lax.div(model, 2)
        self.core = lax.rem(model, 2)
        self.group = self.y * 2 + self.z

    def at(self, dx=0, dy=0, dz=0, dhigh=0, dcore=0):
        x = lax.rem(self.x + dx, 4)
        y = lax.rem(self.y + dy, 4)
        z = lax.rem(self.z + dz, 2)
        high = lax.rem(self.high + dhigh, 2)
        core = lax.rem(self.core + dcore, 2)
        return (x * 8 + y * 2 + z, high * 2 + core)


class Links:
    def __init__(self, send_sem, recv_sem):
        self.send_sem, self.recv_sem = send_sem, recv_sem
        self.used = 0
        self.sent = []

    def copy(self, source, target, device):
        at = self.used
        self.used += 1
        made = pltpu.make_async_remote_copy(
            src_ref=source,
            dst_ref=target,
            send_sem=self.send_sem.at[at],
            recv_sem=self.recv_sem.at[at],
            device_id=device,
            device_id_type=MESH,
        )
        self.sent.append(made)
        return made

    def send(self, source, target, device):
        made = self.copy(source, target, device)
        made.start()
        return made

    def finish(self):
        for made in self.sent:
            made.wait_send()
        self.sent = []


def greet(partners):
    barrier = pltpu.get_barrier_semaphore()
    for device in partners:
        pl.semaphore_signal(barrier, inc=1, device_id=device, device_id_type=MESH)
    return lambda: pl.semaphore_wait(barrier, len(partners))


def all_partners(me):
    return [
        me.at(dx=1), me.at(dx=3), me.at(dx=2), me.at(dy=1), me.at(dy=3),
        me.at(dz=1), me.at(dhigh=1), me.at(dcore=1),
    ]


def row_norm(values):
    mean = jnp.mean(values, axis=-1, keepdims=True)
    centred = values - mean
    variance = jnp.mean(centred * centred, axis=-1, keepdims=True)
    inverse = lax.rsqrt(variance + EPSILON)
    return centred * inverse, inverse


def spread(column):
    return jnp.broadcast_to(column, (column.shape[0], 128))


class Gather:
    def __init__(self, me, links, slots, rows):
        self.me, self.links, self.slots = me, links, slots
        self.low = pl.ds(0, rows // 2)
        self.high = pl.ds(rows // 2, rows // 2)
        self.other = 1 - me.z

    def slot(self, dy, z):
        return lax.rem(self.me.y + dy, 4) * 2 + z

    def send(self, slot, device):
        return self.links.send(self.slots.at[slot], self.slots.at[slot], device)

    def begin(self):
        me = self.me
        own = me.group
        self.from_z = self.send(own, me.at(dz=1))
        self.own_y = [self.send(own, me.at(dy=1)), self.send(own, me.at(dy=3))]

    def pass_z(self):
        me = self.me
        self.from_z.wait_recv()
        slot = self.slot(0, self.other)
        self.other_y = [self.send(slot, me.at(dy=1)), self.send(slot, me.at(dy=3))]

    def forward(self, pair, z):
        me = self.me
        pair[0].wait_recv()
        below = self.slot(3, z)
        up = self.links.send(
            self.slots.at[below, self.low], self.slots.at[below, self.low], me.at(dy=1)
        )
        pair[1].wait_recv()
        above = self.slot(1, z)
        down = self.links.send(
            self.slots.at[above, self.high], self.slots.at[above, self.high], me.at(dy=3)
        )
        return [up, down]

    def pass_own(self):
        self.far_own = self.forward(self.own_y, self.me.z)

    def pass_other(self):
        self.far_other = self.forward(self.other_y, self.other)

    def end_own(self):
        for made in self.far_own:
            made.wait_recv()

    def end_other(self):
        for made in self.far_other:
            made.wait_recv()


def attention_kernel(
    x_ref, gain_ref, shift_ref, weight_ref, bias_ref, output_ref, image_ref,
    first_out, kv_out, query_out, mixed_out, stats_out, attended_out, output_out,
    kv, query_pair, kv_send, query_send, query_own, top, total, mixed,
    head_send, head_recv, attended, output_all, send_sem, recv_sem,
):
    me = Place()
    links = Links(send_sem, recv_sem)
    wait_all = greet(all_partners(me))

    normed, _ = row_norm(x_ref[...])
    first_low = (normed * gain_ref[...] + shift_ref[...]).astype(BF16)
    first_out[...] = first_low
    keys = dot_nn(first_low, weight_ref[1])
    values = dot_nn(first_low, weight_ref[2]) + bias_ref[1:2, :]
    for head in range(4):
        part = slice(head * HEAD_DIM, (head + 1) * HEAD_DIM)
        kv_send[head] = jnp.concatenate([keys[:, part], values[:, part]], axis=1).astype(BF16)
    queries = dot_nn(first_low, weight_ref[0]) + bias_ref[0:1, :]
    queries = queries.astype(BF16).astype(F32) * (HEAD_DIM**-0.5)
    for head in range(4):
        part = slice(head * HEAD_DIM, (head + 1) * HEAD_DIM)
        query_send[head] = jnp.concatenate(
            [queries[:128, part], queries[128:, part]], axis=1
        ).astype(BF16)

    wait_all()
    own = me.group
    kv_moves, query_moves = [], []
    for step in (1, 3, 2):
        head = lax.rem(me.x + step, 4)
        kv_moves.append(
            links.send(kv_send.at[head], kv.at[own, pl.ds(me.x * 256, 256)], me.at(dx=step))
        )
    for step in (1, 3, 2):
        head = lax.rem(me.x + step, 4)
        query_moves.append(
            links.send(
                query_send.at[head], query_pair.at[own, pl.ds(me.x * 128, 128)], me.at(dx=step)
            )
        )
    kv[own, pl.ds(me.x * 256, 256), :] = kv_send[me.x]
    query_pair[own, pl.ds(me.x * 128, 128), :] = query_send[me.x]
    attended_at = me.high * 2 + me.core

    for made in kv_moves:
        made.wait_recv()
    gather = Gather(me, links, kv, 1024)
    gather.begin()
    output_all[attended_at] = output_ref[...]
    output_high = links.send(output_ref, output_all.at[attended_at], me.at(dhigh=1))
    output_core = links.send(output_ref, output_all.at[attended_at], me.at(dcore=1))
    for made in query_moves:
        made.wait_recv()
    for block in range(4):
        pair = query_pair[own, block * 128 : (block + 1) * 128, :].astype(F32)
        both = jnp.concatenate([pair, pltpu.roll(pair, 64, 1)], axis=0)
        lane = lax.broadcasted_iota(jnp.int32, both.shape, 1)
        query_own[block * 256 : (block + 1) * 256, :] = jnp.where(
            lane < HEAD_DIM, both, 0.0
        ).astype(BF16)
    query_gather = Gather(me, links, query_pair, 512)
    top[...] = jnp.full(top.shape, LOWEST, F32)
    total[...] = jnp.zeros(total.shape, F32)
    mixed[...] = jnp.zeros(mixed.shape, F32)

    def attend(slot):
        @pl.loop(0, 4)
        def _(block):
            rows = pl.ds(pl.multiple_of(block * 256, 256), 256)
            query = query_own[rows, :]
            mine = image_ref[block * 8 + own]
            scores, shut = [], []
            highest = None
            for part in range(4):
                same = image_ref[part * 8 + slot] == mine
                shut.append(jnp.where(same, -3e38, HIGHEST))
                score = dot_nt(query, kv[slot, part * 256 : (part + 1) * 256, :])
                scores.append(score)
                peak = jnp.maximum(score[:, :128], score[:, 128:])
                peak = jnp.minimum(peak, jnp.where(same, 3e38, LOWEST))
                highest = peak if highest is None else jnp.maximum(highest, peak)
            before = top[rows, :]
            now = jnp.maximum(before, spread(jnp.max(highest, axis=1, keepdims=True)))
            fade = jnp.exp(before - now)
            top[rows, :] = now
            sums = total[rows, :] * fade
            acc = mixed[rows, :] * fade
            for part in range(4):
                level = jnp.maximum(now, shut[part])
                prob = jnp.exp(scores[part] - jnp.concatenate([level, level], axis=1))
                sums = sums + prob[:, :128] + prob[:, 128:]
                acc = acc + dot_nn(prob.astype(BF16), kv[slot, part * 256 : (part + 1) * 256, :])
            total[rows, :] = sums
            mixed[rows, :] = acc

    attend(own)
    gather.pass_z()
    attend(gather.slot(0, gather.other))
    gather.pass_own()
    query_gather.begin()
    attend(gather.slot(3, me.z))
    attend(gather.slot(1, me.z))
    gather.pass_other()
    query_gather.pass_z()
    attend(gather.slot(3, gather.other))
    attend(gather.slot(1, gather.other))
    output_high.wait_recv()
    across = lax.rem(me.high + 1, 2) * 2 + me.core
    output_pass = links.send(output_all.at[across], output_all.at[across], me.at(dcore=1))
    gather.end_own()
    attend(gather.slot(2, me.z))
    gather.end_other()
    attend(gather.slot(2, gather.other))

    for block in range(4):
        rows = slice(block * 256, (block + 1) * 256)
        sums = spread(jnp.sum(total[rows, :], axis=1, keepdims=True))
        out = mixed[rows, :] / sums
        mixed[rows, :] = out
        log_total = top[rows, :] + jnp.log(sums)
        stats_out[block : block + 1, :] = log_total.T[0:1, :]
        back = pltpu.roll(out[:128, :], 64, 1)
        lane = lax.broadcasted_iota(jnp.int32, back.shape, 1)
        head_send[block] = jnp.where(lane < HEAD_DIM, back, out[128:, :]).astype(BF16)
    stats_out[4:, :] = jnp.zeros((4, 256), F32)
    head_moves = []
    for step in (1, 3, 2):
        to = lax.rem(me.x + step, 4)
        head_moves.append(links.send(head_send.at[to], head_recv.at[me.x], me.at(dx=step)))
    head_recv[me.x] = head_send[me.x]
    query_gather.pass_own()
    for made in head_moves:
        made.wait_recv()
    upper = jnp.concatenate([head_recv[head].astype(F32)[:, :64] for head in range(4)], axis=1)
    lower = jnp.concatenate([head_recv[head].astype(F32)[:, 64:] for head in range(4)], axis=1)
    attended[attended_at] = jnp.concatenate([upper, lower], axis=0).astype(BF16)
    here = attended.at[attended_at]
    attended_high = links.send(here, here, me.at(dhigh=1))
    attended_core = links.send(here, here, me.at(dcore=1))
    query_gather.pass_other()
    mixed_out[...] = mixed[...]
    kv_out[...] = kv[...]
    output_core.wait_recv()
    output_pass.wait_recv()
    output_out[...] = output_all[...]
    attended_high.wait_recv()
    attended_pass = links.send(attended.at[across], attended.at[across], me.at(dcore=1))
    query_gather.end_own()
    query_gather.end_other()
    query_out[...] = query_pair[...]
    attended_core.wait_recv()
    attended_pass.wait_recv()
    attended_out[...] = attended[...]
    links.finish()


def attention(x, gain, shift, weight, bias, output_weight, image_of):
    vmem = pl.BlockSpec(memory_space=pltpu.VMEM)
    return pl.pallas_call(
        attention_kernel,
        out_shape=[
            jax.ShapeDtypeStruct((256, 1024), BF16),
            jax.ShapeDtypeStruct((8, 1024, 128), BF16),
            jax.ShapeDtypeStruct((8, 512, 128), BF16),
            jax.ShapeDtypeStruct((1024, 128), F32),
            jax.ShapeDtypeStruct((8, 256), F32),
            jax.ShapeDtypeStruct((4, 256, 256), BF16),
            jax.ShapeDtypeStruct((4, 256, 1024), BF16),
        ],
        in_specs=[vmem] * 6 + [pl.BlockSpec(memory_space=pltpu.SMEM)],
        out_specs=[vmem] * 7,
        scratch_shapes=[
            pltpu.VMEM((8, 1024, 128), BF16),
            pltpu.VMEM((8, 512, 128), BF16),
            pltpu.VMEM((4, 256, 128), BF16),
            pltpu.VMEM((4, 128, 128), BF16),
            pltpu.VMEM((1024, 128), BF16),
            pltpu.VMEM((1024, 128), F32),
            pltpu.VMEM((1024, 128), F32),
            pltpu.VMEM((1024, 128), F32),
            pltpu.VMEM((4, 128, 128), BF16),
            pltpu.VMEM((4, 128, 128), BF16),
            pltpu.VMEM((4, 256, 256), BF16),
            pltpu.VMEM((4, 256, 1024), BF16),
            pltpu.SemaphoreType.DMA((40,)),
            pltpu.SemaphoreType.DMA((40,)),
        ],
        compiler_params=pltpu.CompilerParams(
            collective_id=0, has_side_effects=True, vmem_limit_bytes=VMEM_BYTES
        ),
    )(x, gain, shift, weight, bias, output_weight, image_of)


class ModelSum:
    def __init__(self, me, links, part, pair, half, far, full):
        self.me, self.links = me, links
        self.part, self.pair, self.half, self.far, self.full = part, pair, half, far, full
        self.own = pl.ds(pl.multiple_of(me.core * 128, 128), 128)
        self.other = pl.ds(pl.multiple_of((1 - me.core) * 128, 128), 128)

    def fill(self, rows, tile):
        @pl.loop(0, 4)
        def _(step):
            cols = pl.ds(pl.multiple_of(step * 256, 256), 256)
            self.part[rows, cols] = tile(rows, cols).astype(BF16)

    def begin(self, tile):
        self.fill(self.other, tile)
        self.first = self.links.send(self.part.at[self.other], self.pair, self.me.at(dcore=1))
        self.fill(self.own, tile)

    def cross(self):
        self.first.wait_recv()
        self.half[...] = (self.part[self.own, :].astype(F32) + self.pair[...].astype(F32)).astype(BF16)
        self.second = self.links.send(self.half, self.far, self.me.at(dhigh=1))

    def back(self):
        self.second.wait_recv()
        self.full[self.own, :] = (self.half[...].astype(F32) + self.far[...].astype(F32)).astype(BF16)
        self.third = self.links.send(
            self.full.at[self.own], self.full.at[self.own], self.me.at(dcore=1)
        )

    def end(self):
        self.third.wait_recv()


def ring(me, axis):
    if axis == "x":
        return me.x, me.at(dx=1), me.at(dx=3)
    return me.y, me.at(dy=1), me.at(dy=3)


def add_rows(target, rows, cols, count, sources):
    step = min(count, 64)

    @pl.loop(0, count // step)
    def _(index):
        here = pl.ds(pl.multiple_of(index * step, step), step)
        there = pl.ds(pl.multiple_of(rows + index * step, step), step)
        value = target[there, cols].astype(F32)
        for source in sources:
            value = value + source[here, :].astype(F32)
        target[there, cols] = value.astype(BF16)


def weight_sum(me, links, axes, parts, whole, stages, cross, result, done_sem):
    height, width = parts.shape
    low, high = pl.ds(0, width // 2), pl.ds(width // 2, width // 2)
    base, count = 0, height
    bases = []
    for axis, (side_up, side_down, main_up, main_down) in zip(axes, stages):
        spot, up, down = ring(me, axis)
        count = count // 4
        bases.append((base, count))

        def chunk(step, base=base, spot=spot, count=count):
            return pl.multiple_of(base + lax.rem(spot + step, 4) * count, 16)

        def rows(step, count=count, chunk=chunk):
            return pl.ds(chunk(step), count)

        far_up = links.send(parts.at[rows(2), low], side_up, up)
        far_down = links.send(parts.at[rows(2), high], side_down, down)
        near = [
            links.send(parts.at[rows(1), high], main_up.at[:, high], up),
            links.send(parts.at[rows(3), low], main_down.at[:, low], down),
        ]
        yield
        far_up.wait_recv()
        add_rows(parts, chunk(1), low, count, [side_up])
        near.append(links.send(parts.at[rows(1), low], main_up.at[:, low], up))
        far_down.wait_recv()
        add_rows(parts, chunk(3), high, count, [side_down])
        near.append(links.send(parts.at[rows(3), high], main_down.at[:, high], down))
        yield
        for made in near:
            made.wait_recv()
        base = chunk(0)
        add_rows(parts, base, slice(None), count, [main_up, main_down])
    rows = pl.ds(base, count)
    own = pl.ds(pl.multiple_of(me.z * (width // 2), 128), width // 2)
    other = pl.ds(pl.multiple_of((1 - me.z) * (width // 2), 128), width // 2)
    made = links.send(parts.at[rows, other], cross, me.at(dz=1))
    yield
    made.wait_recv()
    whole[rows, own] = (parts[rows, own].astype(F32) + cross[...].astype(F32)).astype(BF16)
    made = links.send(whole.at[rows, own], whole.at[rows, own], me.at(dz=1))
    yield
    made.wait_recv()
    for axis, (base, count) in zip(axes[::-1], bases[::-1]):
        spot, up, down = ring(me, axis)

        def rows(step, base=base, spot=spot, count=count):
            return pl.ds(pl.multiple_of(base + lax.rem(spot + step, 4) * count, 16), count)

        mine = whole.at[rows(0)]
        above = links.send(mine, mine, up)
        below = links.send(mine, mine, down)
        yield
        above.wait_recv()
        piece = whole.at[rows(3), low]
        far = [links.send(piece, piece, up)]
        below.wait_recv()
        piece = whole.at[rows(1), high]
        far.append(links.send(piece, piece, down))
        yield
        for made in far:
            made.wait_recv()
    copy = pltpu.make_async_copy(whole, result, done_sem)
    copy.start()
    yield
    copy.wait()


def vector_sum(me, links, values, from_z, along_x, along_y):
    made = links.send(values, from_z, me.at(dz=1))
    yield
    made.wait_recv()
    for slots, spot, name in ((along_x, me.x, "dx"), (along_y, me.y, "dy")):
        if name == "dx":
            slots[spot] = values[...] + from_z[...]
        else:
            slots[spot] = along_x[0] + along_x[1] + along_x[2] + along_x[3]
        here = slots.at[spot]
        moves = [links.send(here, here, me.at(**{name: step})) for step in (1, 3, 2)]
        yield
        for made in moves:
            made.wait_recv()


def advance(jobs):
    for job in list(jobs):
        try:
            next(job)
        except StopIteration:
            jobs.remove(job)


def lanes_below(shape):
    return lax.broadcasted_iota(jnp.int32, shape, 1) < HEAD_DIM


def pack_rows(values):
    return jnp.where(lanes_below((128, 128)), values[:128, :], pltpu.roll(values[128:, :], 64, 1))


def backward_kernel(
    x_ref, cot_ref, gain_one_ref, first_ref, kv_ref, query_ref, mixed_ref, stats_ref,
    attended_ref, output_ref, output_bias_ref, gain_two_ref, shift_two_ref,
    up_ref, up_bias_ref, down_ref, down_bias_ref, weight_ref, mates_ref, count_ref,
    result_out, input_out, vector_out, up_out, down_out, qk_out, v_out, o_out,
    hidden, xhat_two, inverse_two, second_low, down_grad, activated, pre_grad,
    branch_low, sums, units, lows,
    grad_send, grad_pair, stats_all, query_own, grad_own, levels, rows_all, query_grad_all,
    acc_one, acc_two, qg_send, qg_recv, kvg_send, kvg_recv, stacked,
    vector, from_z, along_x, along_y,
    jobs_up, jobs_down, jobs_qk, jobs_v, jobs_o,
    send_sem, recv_sem, done_sem,
):
    me = Place()
    links = Links(send_sem, recv_sem)
    wait_all = greet(all_partners(me))
    own = me.group
    column_tiles = 4

    def cols_of(step):
        return pl.ds(pl.multiple_of(step * 256, 256), 256)

    @pl.loop(0, column_tiles)
    def _(step):
        cols = cols_of(step)
        value = x_ref[:, cols] + output_bias_ref[:, cols]
        for part in range(4):
            value = value + dot_nn(attended_ref[part], output_ref[part, :, cols])
        hidden[:, cols] = value

    normed, inverse = row_norm(hidden[...])
    xhat_two[...] = normed
    inverse_two[...] = spread(inverse)
    second_low[...] = (normed * gain_two_ref[...] + shift_two_ref[...]).astype(BF16)
    down_grad[...] = cot_ref[...].astype(BF16)

    @pl.loop(0, column_tiles)
    def _(step):
        cols = cols_of(step)
        pre = dot_nn(second_low[...], up_ref[:, cols]) + up_bias_ref[:, cols]
        back = dot_nt(down_grad[...], down_ref[cols, :])
        spread_of = 0.5 + 0.5 * lax.erf(pre * (0.5**0.5))
        density = jnp.exp(-0.5 * pre * pre) * 0.3989422804014327
        activated[:, cols] = (pre * spread_of).astype(BF16)
        low = (back * (spread_of + pre * density)).astype(BF16)
        pre_grad[:, cols] = low
        vector[4:5, cols] = jnp.sum(low.astype(F32), axis=0, keepdims=True)

    wait_all()
    norm_sum = ModelSum(me, links, *sums)
    norm_sum.begin(lambda rows, cols: dot_nt(pre_grad[rows, :], up_ref[cols, :]))
    norm_sum.cross()

    up_parts, down_parts = jobs_up[0], jobs_down[0]

    @pl.loop(0, column_tiles)
    def _(step):
        cols = cols_of(step)
        up_parts[cols, :] = dot_tn(second_low[:, cols], pre_grad[...]).astype(BF16)

    jobs = []
    jobs.append(weight_sum(me, links, "xy", *jobs_up, up_out, done_sem.at[0]))

    @pl.loop(0, column_tiles)
    def _(step):
        cols = cols_of(step)
        down_parts[cols, :] = dot_tn(activated[:, cols], down_grad[...]).astype(BF16)

    jobs.append(weight_sum(me, links, "yx", *jobs_down, down_out, done_sem.at[1]))
    advance(jobs)
    unit_sum = ModelSum(me, links, *units)
    unit_sum.begin(lambda rows, cols: dot_nn(activated[rows, :], down_ref[:, cols]))
    vector[3:4, :] = jnp.sum(down_grad[...].astype(F32), axis=0, keepdims=True)
    norm_sum.back()
    unit_sum.cross()
    norm_sum.end()

    grad = norm_sum.full[...].astype(F32)
    xhat = xhat_two[...]
    vector[0:1, :] = jnp.sum(grad * xhat, axis=0, keepdims=True)
    vector[1:2, :] = jnp.sum(grad, axis=0, keepdims=True)
    scaled = grad * gain_two_ref[...]
    hidden_grad = cot_ref[...] + (
        scaled
        - jnp.mean(scaled, axis=-1, keepdims=True)
        - xhat * jnp.mean(scaled * xhat, axis=-1, keepdims=True)
    ) * inverse_two[:, 0:1]
    input_out[...] = hidden_grad
    low = hidden_grad.astype(BF16)
    branch_low[...] = low
    vector[2:3, :] = jnp.sum(low.astype(F32), axis=0, keepdims=True)

    at = me.high * 2 + me.core
    attended_grad = dot_nt(branch_low[...], output_ref[at]).astype(BF16).astype(F32)
    for head in range(4):
        part = slice(head * HEAD_DIM, (head + 1) * HEAD_DIM)
        grad_send[head] = jnp.concatenate(
            [attended_grad[:128, part], attended_grad[128:, part]], axis=1
        ).astype(BF16)
    moves = []
    for step in (1, 3, 2):
        head = lax.rem(me.x + step, 4)
        moves.append(links.send(grad_send.at[head], grad_pair.at[own, me.x], me.at(dx=step)))
    grad_pair[own, me.x] = grad_send[me.x]

    o_parts = jobs_o[0]

    @pl.loop(0, column_tiles)
    def _(step):
        cols = cols_of(step)
        o_parts[:, cols] = dot_tn(attended_ref[at], branch_low[:, cols]).astype(BF16)

    for made in moves:
        made.wait_recv()
    gather = Gather(me, links, grad_pair, 4)
    gather.begin()
    stats_all[own] = stats_ref[...]

    @pl.loop(0, 4)
    def _(block):
        pair = query_ref[own * 4 + block].astype(F32)
        both = jnp.concatenate([pair, pltpu.roll(pair, 64, 1)], axis=0)
        keep = lanes_below(both.shape)
        query_own[block] = jnp.where(keep, both, 0.0).astype(BF16)
        pair = grad_pair[own, block].astype(F32)
        both = jnp.concatenate([pltpu.roll(pair, 64, 1), pair], axis=0)
        both = jnp.where(keep, 0.0, both)
        grad_own[block] = both.astype(BF16)
        delta = spread(jnp.sum(both * mixed_ref[block], axis=1, keepdims=True))
        levels[block, 1] = delta
        stats_all[own, pl.ds(block + 4, 1), :] = delta.T[0:1, :]
        line = stats_ref[pl.ds(block, 1), :]
        levels[block, 0] = jnp.broadcast_to(line, (128, 256)).T

    stats_gather = Gather(me, links, stats_all, 8)
    stats_gather.begin()

    def wide(value):
        return jnp.concatenate([value, value], axis=1)

    def query_pass(block):
        query, grad_out = query_own[block], grad_own[block]
        line = block * 8 + own
        acc_one[...] = jnp.zeros(acc_one.shape, F32)

        @pl.loop(0, 4)
        def _(step):
            acc = acc_one[...]
            for part in range(4):
                index = step * 4 + part
                shut = jnp.where(index < count_ref[line], -3e38, HIGHEST)
                keys = kv_ref[mates_ref[line * 16 + index]]
                level = jnp.maximum(levels[block, 0], shut)
                prob = jnp.exp(dot_nt(query, keys) - wide(level))
                change = prob * (dot_nt(grad_out, keys) - wide(levels[block, 1]))
                acc = acc + dot_nn(change.astype(BF16), keys)
            acc_one[...] = acc

        qg_send[block] = pack_rows(acc_one[...] * (HEAD_DIM**-0.5)).astype(BF16)

    query_moves = []

    def send_query(step):
        block = lax.rem(me.x + step, 4)
        query_pass(block)
        if step:
            query_moves.append(
                links.send(qg_send.at[block], qg_recv.at[me.x], me.at(dx=step))
            )

    send_query(2)
    gather.pass_z()
    stats_gather.pass_z()
    advance(jobs)
    send_query(1)
    gather.pass_own()
    stats_gather.pass_own()
    unit_sum.back()
    advance(jobs)
    send_query(3)
    gather.pass_other()
    stats_gather.pass_other()
    unit_sum.end()
    result_out[...] = hidden[...] + unit_sum.full[...].astype(F32) + down_bias_ref[...]
    advance(jobs)
    jobs.append(weight_sum(me, links, "yx", *jobs_o, o_out, done_sem.at[4]))
    send_query(0)
    qg_recv[me.x] = qg_send[me.x]
    advance(jobs)
    gather.end_own()
    gather.end_other()
    stats_gather.end_own()
    stats_gather.end_other()

    @pl.loop(0, 32)
    def _(spot):
        slot, block = lax.div(spot, 4), lax.rem(spot, 4)
        pair = query_ref[spot].astype(F32)
        other = grad_pair[slot, block].astype(F32)
        keep = lanes_below(pair.shape)
        upper = jnp.where(keep, pair, pltpu.roll(other, 64, 1))
        lower = jnp.where(keep, pltpu.roll(pair, 64, 1), other)
        query_grad_all[spot] = jnp.concatenate([upper, lower], axis=0).astype(BF16)
        rows_all[spot, 0:1, :] = stats_all[slot, pl.ds(block, 1), :]
        rows_all[spot, 1:2, :] = stats_all[slot, pl.ds(block + 4, 1), :]

    def key_pass(block):
        both = kv_ref[own * 4 + block].astype(F32)
        keep = lanes_below(both.shape)
        key = jnp.where(keep, both, 0.0).astype(BF16)
        value = jnp.where(keep, 0.0, both).astype(BF16)
        line = block * 8 + own
        acc_one[...] = jnp.zeros(acc_one.shape, F32)
        acc_two[...] = jnp.zeros(acc_two.shape, F32)

        @pl.loop(0, 4)
        def _(step):
            key_acc, value_acc = acc_one[...], acc_two[...]
            for part in range(4):
                index = step * 4 + part
                shut = jnp.where(index < count_ref[line], -3e38, HIGHEST)
                spot = mates_ref[line * 16 + index]
                pair = query_grad_all[spot]
                lines = rows_all[spot]
                prob = jnp.exp(dot_nt(key, pair) - jnp.maximum(lines[0:1, :], shut))
                change = prob * (dot_nt(value, pair) - lines[1:2, :])
                value_acc = value_acc + dot_nn(prob.astype(BF16), pair)
                key_acc = key_acc + dot_nn(change.astype(BF16), pair)
            acc_one[...] = key_acc
            acc_two[...] = value_acc

        kvg_send[block] = jnp.where(keep, acc_one[...], acc_two[...]).astype(BF16)

    key_moves = []
    for step in (2, 1, 3, 0):
        block = lax.rem(me.x + step, 4)
        key_pass(block)
        if step:
            key_moves.append(links.send(kvg_send.at[block], kvg_recv.at[me.x], me.at(dx=step)))
        advance(jobs)
    kvg_recv[me.x] = kvg_send[me.x]
    for made in query_moves + key_moves:
        made.wait_recv()

    heads = [qg_recv[head].astype(F32) for head in range(4)]
    upper = jnp.concatenate([value[:, :64] for value in heads], axis=1)
    lower = jnp.concatenate([value[:, 64:] for value in heads], axis=1)
    stacked[:, 0:256] = jnp.concatenate([upper, lower], axis=0).astype(BF16)
    heads = [kvg_recv[head].astype(F32) for head in range(4)]
    stacked[:, 256:512] = jnp.concatenate([value[:, :64] for value in heads], axis=1).astype(BF16)
    stacked[:, 512:768] = jnp.concatenate([value[:, 64:] for value in heads], axis=1).astype(BF16)
    vector[5:6, 0:256] = jnp.sum(stacked[:, 0:256].astype(F32), axis=0, keepdims=True)
    vector[5:6, 256:512] = jnp.sum(stacked[:, 512:768].astype(F32), axis=0, keepdims=True)
    vector[5:6, 512:1024] = jnp.zeros((1, 512), F32)
    low_sum = ModelSum(me, links, *lows)
    low_sum.begin(
        lambda rows, cols: dot_nt(stacked[rows, 0:256], weight_ref[0, cols, :])
        + dot_nt(stacked[rows, 256:512], weight_ref[1, cols, :])
        + dot_nt(stacked[rows, 512:768], weight_ref[2, cols, :])
    )
    low_sum.cross()
    qk_parts, v_parts = jobs_qk[0], jobs_v[0]

    @pl.loop(0, column_tiles)
    def _(step):
        cols = cols_of(step)
        value = dot_tn(first_ref[:, cols], stacked[...]).astype(BF16)
        qk_parts[cols, :] = value[:, 0:512]
        v_parts[cols, :] = value[:, 512:768]

    jobs.append(weight_sum(me, links, "xy", *jobs_qk, qk_out, done_sem.at[2]))
    jobs.append(weight_sum(me, links, "yx", *jobs_v, v_out, done_sem.at[3]))
    advance(jobs)
    low_sum.back()
    advance(jobs)
    low_sum.end()
    grad = low_sum.full[...].astype(F32)
    xhat, inverse = row_norm(x_ref[...])
    vector[6:7, :] = jnp.sum(grad * xhat, axis=0, keepdims=True)
    vector[7:8, :] = jnp.sum(grad, axis=0, keepdims=True)
    jobs.append(vector_sum(me, links, vector, from_z, along_x, along_y))
    advance(jobs)
    scaled = grad * gain_one_ref[...]
    input_out[...] = input_out[...] + (
        scaled
        - jnp.mean(scaled, axis=-1, keepdims=True)
        - xhat * jnp.mean(scaled * xhat, axis=-1, keepdims=True)
    ) * inverse
    while jobs:
        advance(jobs)
    vector_out[...] = along_y[0] + along_y[1] + along_y[2] + along_y[3]
    links.finish()


def job_scratch(height, width):
    shapes = []
    stages = []
    count = height
    for _ in range(2):
        count = count // 4
        stages.append(
            [
                pltpu.VMEM((count, width // 2), BF16),
                pltpu.VMEM((count, width // 2), BF16),
                pltpu.VMEM((count, width), BF16),
                pltpu.VMEM((count, width), BF16),
            ]
        )
    return [
        pltpu.VMEM((height, width), BF16),
        pltpu.VMEM((height, width), BF16),
        stages,
        pltpu.VMEM((count, width // 2), BF16),
    ]


def sum_scratch():
    return [
        pltpu.VMEM((256, 1024), BF16),
        pltpu.VMEM((128, 1024), BF16),
        pltpu.VMEM((128, 1024), BF16),
        pltpu.VMEM((128, 1024), BF16),
        pltpu.VMEM((256, 1024), BF16),
    ]


def backward(*args):
    vmem = pl.BlockSpec(memory_space=pltpu.VMEM)
    smem = pl.BlockSpec(memory_space=pltpu.SMEM)
    hbm = pl.BlockSpec(memory_space=pl.ANY)
    return pl.pallas_call(
        backward_kernel,
        out_shape=[
            jax.ShapeDtypeStruct((256, 1024), F32),
            jax.ShapeDtypeStruct((256, 1024), F32),
            jax.ShapeDtypeStruct((8, 1024), F32),
            jax.ShapeDtypeStruct((1024, 1024), BF16),
            jax.ShapeDtypeStruct((1024, 1024), BF16),
            jax.ShapeDtypeStruct((1024, 512), BF16),
            jax.ShapeDtypeStruct((1024, 256), BF16),
            jax.ShapeDtypeStruct((256, 1024), BF16),
        ],
        in_specs=[vmem] * 18 + [smem] * 2,
        out_specs=[vmem] * 3 + [hbm] * 5,
        scratch_shapes=[
            pltpu.VMEM((256, 1024), F32),
            pltpu.VMEM((256, 1024), F32),
            pltpu.VMEM((256, 128), F32),
            pltpu.VMEM((256, 1024), BF16),
            pltpu.VMEM((256, 1024), BF16),
            pltpu.VMEM((256, 1024), BF16),
            pltpu.VMEM((256, 1024), BF16),
            pltpu.VMEM((256, 1024), BF16),
            sum_scratch(),
            sum_scratch(),
            sum_scratch(),
            pltpu.VMEM((4, 128, 128), BF16),
            pltpu.VMEM((8, 4, 128, 128), BF16),
            pltpu.VMEM((8, 8, 256), F32),
            pltpu.VMEM((4, 256, 128), BF16),
            pltpu.VMEM((4, 256, 128), BF16),
            pltpu.VMEM((4, 2, 256, 128), F32),
            pltpu.VMEM((32, 8, 256), F32),
            pltpu.VMEM((32, 256, 128), BF16),
            pltpu.VMEM((256, 128), F32),
            pltpu.VMEM((256, 128), F32),
            pltpu.VMEM((4, 128, 128), BF16),
            pltpu.VMEM((4, 128, 128), BF16),
            pltpu.VMEM((4, 256, 128), BF16),
            pltpu.VMEM((4, 256, 128), BF16),
            pltpu.VMEM((256, 768), BF16),
            pltpu.VMEM((8, 1024), F32),
            pltpu.VMEM((8, 1024), F32),
            pltpu.VMEM((4, 8, 1024), F32),
            pltpu.VMEM((4, 8, 1024), F32),
            job_scratch(1024, 1024),
            job_scratch(1024, 1024),
            job_scratch(1024, 512),
            job_scratch(1024, 256),
            job_scratch(256, 1024),
            pltpu.SemaphoreType.DMA((170,)),
            pltpu.SemaphoreType.DMA((170,)),
            pltpu.SemaphoreType.DMA((5,)),
        ],
        compiler_params=pltpu.CompilerParams(
            collective_id=1, has_side_effects=True, vmem_limit_bytes=VMEM_BYTES
        ),
    )(*args)


def per_device(
    inputs,
    first_gain,
    first_shift,
    attend_weight,
    attend_bias,
    output_weight,
    output_bias,
    second_gain,
    second_shift,
    up_weight,
    up_bias,
    down_weight,
    down_bias,
    image_of,
    cotangent,
):
    first_low, kv, query_pair, mixed, stats, attended, output_all = attention(
        inputs, first_gain[None], first_shift[None], attend_weight, attend_bias, output_weight, image_of
    )
    same = image_of[:, None] == image_of[None, :]
    index = jnp.arange(32)
    rank = jnp.sum(same[:, None, :] & (index[None, :] < index[:, None])[None], axis=2)
    place = (index % 8) * 4 + index // 8
    chosen = same[:, None, :] & (rank[:, None, :] == jnp.arange(16)[None, :, None])
    mates = jnp.sum(jnp.where(chosen, place[None, None, :], 0), axis=2).astype(jnp.int32)
    count = jnp.sum(same, axis=1).astype(jnp.int32)
    result, input_grad, vector, up, down, qk, v, o = backward(
        inputs, cotangent, first_gain[None], first_low, kv.reshape(32, 256, 128),
        query_pair.reshape(32, 128, 128), mixed.reshape(4, 256, 128), stats,
        attended, output_all, output_bias[None], second_gain[None], second_shift[None],
        up_weight, up_bias[None], down_weight, down_bias[None], attend_weight,
        mates.reshape(512), count,
    )
    weight_grad = jnp.stack([qk[:, :256], qk[:, 256:], v]).astype(F32)
    return (
        result, input_grad, vector[6], vector[7], weight_grad,
        vector[5, :512].reshape(2, 256), o.astype(F32), vector[2], vector[0], vector[1],
        up.astype(F32), vector[4], down.astype(F32), vector[3],
    )


def solution(mesh):
    in_specs = (
        P("dp", None), P(), P(), P(None, None, "mp"), P(None, "mp"), P("mp", None), P(), P(), P(),
        P(None, "mp"), P("mp"), P("mp", None), P(), P(), P("dp", None),
    )
    out_specs = (
        P("dp", None), P("dp", None), P(), P(), P(None, None, "mp"), P(None, "mp"), P("mp", None),
        P(), P(), P(), P(None, "mp"), P("mp"), P("mp", None), P(),
    )
    return jax.shard_map(
        per_device, mesh=mesh, in_specs=in_specs, out_specs=out_specs, check_vma=False
    )
```

```python
import functools

import jax
import jax.numpy as jnp
from jax import lax
from jax.experimental import pallas as pl
from jax.experimental.pallas import tpu as pltpu
from jax.sharding import PartitionSpec as P

HEAD_DIM = 64
EPSILON = 1e-06
LOWEST = -1e30
HIGHEST = 1e30
MESH = pl.DeviceIdType.MESH
F32 = jnp.float32
BF16 = jnp.bfloat16
VMEM_BYTES = 60 * 2**20


def dot_nn(left, right):
    return lax.dot_general(left, right, (((1,), (0,)), ((), ())), preferred_element_type=F32)


def dot_nt(left, right):
    return lax.dot_general(left, right, (((1,), (1,)), ((), ())), preferred_element_type=F32)


def dot_tn(left, right):
    return lax.dot_general(left, right, (((0,), (0,)), ((), ())), preferred_element_type=F32)


class Place:
    def __init__(self):
        data, model = lax.axis_index("dp"), lax.axis_index("mp")
        self.x = lax.div(data, 8)
        self.y = lax.rem(lax.div(data, 2), 4)
        self.z = lax.rem(data, 2)
        self.high = lax.div(model, 2)
        self.core = lax.rem(model, 2)
        self.group = self.y * 2 + self.z

    def at(self, dx=0, dy=0, dz=0, dhigh=0, dcore=0):
        x = lax.rem(self.x + dx, 4)
        y = lax.rem(self.y + dy, 4)
        z = lax.rem(self.z + dz, 2)
        high = lax.rem(self.high + dhigh, 2)
        core = lax.rem(self.core + dcore, 2)
        return (x * 8 + y * 2 + z, high * 2 + core)


class Links:
    def __init__(self, send_sem, recv_sem):
        self.send_sem, self.recv_sem = send_sem, recv_sem
        self.used = 0
        self.sent = []

    def copy(self, source, target, device):
        at = self.used
        self.used += 1
        made = pltpu.make_async_remote_copy(
            src_ref=source,
            dst_ref=target,
            send_sem=self.send_sem.at[at],
            recv_sem=self.recv_sem.at[at],
            device_id=device,
            device_id_type=MESH,
        )
        self.sent.append(made)
        return made

    def send(self, source, target, device):
        made = self.copy(source, target, device)
        made.start()
        return made

    def finish(self):
        for made in self.sent:
            made.wait_send()
        self.sent = []


def greet(partners):
    barrier = pltpu.get_barrier_semaphore()
    for device in partners:
        pl.semaphore_signal(barrier, inc=1, device_id=device, device_id_type=MESH)
    return lambda: pl.semaphore_wait(barrier, len(partners))


def all_partners(me):
    near = [me.at(dx=step) for step in (1, 2, 3)]
    near += [me.at(dx=step, dz=1) for step in (1, 2, 3)]
    near += [me.at(dy=step) for step in (1, 2, 3)]
    near += [me.at(dy=step, dz=1) for step in (1, 2, 3)]
    return near + [me.at(dz=1), me.at(dhigh=1), me.at(dcore=1)]


def row_norm(values):
    mean = jnp.mean(values, axis=-1, keepdims=True)
    centred = values - mean
    variance = jnp.mean(centred * centred, axis=-1, keepdims=True)
    inverse = lax.rsqrt(variance + EPSILON)
    return centred * inverse, inverse


def spread(column):
    return jnp.broadcast_to(column, (column.shape[0], 128))


def wide(value):
    return jnp.concatenate([value, value], axis=1)


def lanes_below(shape):
    return lax.broadcasted_iota(jnp.int32, shape, 1) < HEAD_DIM


def pack_rows(values):
    return jnp.where(lanes_below((128, 128)), values[:128, :], pltpu.roll(values[128:, :], 64, 1))


def pack_heads(values, target):
    for head in range(4):
        part = slice(head * HEAD_DIM, (head + 1) * HEAD_DIM)
        target[head] = jnp.concatenate([values[:128, part], values[128:, part]], axis=1).astype(BF16)


def unpack_heads(source):
    heads = [source[head].astype(F32) for head in range(4)]
    upper = jnp.concatenate([value[:, :HEAD_DIM] for value in heads], axis=1)
    lower = jnp.concatenate([value[:, HEAD_DIM:] for value in heads], axis=1)
    return jnp.concatenate([upper, lower], axis=0).astype(BF16)


class Gather:
    def __init__(self, me, links, blocks):
        self.me, self.links, self.blocks = me, links, blocks
        self.other = 1 - me.z

    def slot(self, dy, z):
        return lax.rem(self.me.y + dy, 4) * 2 + z

    def send(self, slot, first, count, device):
        piece = self.blocks.at[pl.ds(slot * 4 + first, count)]
        return self.links.send(piece, piece, device)

    def begin(self):
        me = self.me
        self.up, self.down, self.across = me.at(dy=1), me.at(dy=3), me.at(dz=1)
        own = me.group
        self.own_y = [self.send(own, 0, 4, self.up), self.send(own, 0, 4, self.down)]
        self.from_z = self.send(own, 0, 4, self.across)

    def pass_z(self):
        self.from_z.wait_recv()
        slot = self.slot(0, self.other)
        self.other_y = [self.send(slot, 0, 2, self.up), self.send(slot, 0, 2, self.down)]

    def pass_own(self):
        below, above = self.slot(3, self.me.z), self.slot(1, self.me.z)
        self.own_y[0].wait_recv()
        self.far_own = [self.send(below, 0, 2, self.up)]
        self.rest = [self.send(below, 2, 2, self.across)]
        self.own_y[1].wait_recv()
        self.far_own.append(self.send(above, 2, 2, self.down))
        self.rest.append(self.send(above, 2, 2, self.across))

    def pass_other(self):
        below, above = self.slot(3, self.other), self.slot(1, self.other)
        self.other_y[0].wait_recv()
        self.far_other = [self.send(below, 0, 1, self.up)]
        self.other_y[1].wait_recv()
        self.far_other.append(self.send(above, 1, 1, self.down))

    def end_near(self):
        for made in self.rest:
            made.wait_recv()

    def end_own(self):
        self.far_own[1].wait_recv()
        self.last = self.send(self.slot(2, self.me.z), 2, 2, self.across)
        self.far_own[0].wait_recv()

    def end_other(self):
        for made in self.far_other + [self.last]:
            made.wait_recv()


class ModelSum:
    def __init__(self, me, links, part, pair, half, far, full):
        self.me, self.links = me, links
        self.part, self.pair, self.half, self.far, self.full = part, pair, half, far, full
        self.own = pl.ds(pl.multiple_of(me.core * 128, 128), 128)
        self.other = pl.ds(pl.multiple_of((1 - me.core) * 128, 128), 128)

    def begin(self, tile):
        @pl.loop(0, 4)
        def _(step):
            cols = cols_of(step)
            self.part[:, cols] = tile(cols).astype(BF16)

        self.first = self.links.send(self.part.at[self.other], self.pair, self.me.at(dcore=1))

    def cross(self):
        self.first.wait_recv()
        self.half[...] = (self.part[self.own, :].astype(F32) + self.pair[...].astype(F32)).astype(BF16)
        self.second = self.links.send(self.half, self.far, self.me.at(dhigh=1))

    def back(self):
        self.second.wait_recv()
        self.full[self.own, :] = (self.half[...].astype(F32) + self.far[...].astype(F32)).astype(BF16)
        self.third = self.links.send(
            self.full.at[self.own], self.full.at[self.own], self.me.at(dcore=1)
        )

    def end(self):
        self.third.wait_recv()


def cols_of(step):
    return pl.ds(pl.multiple_of(step * 256, 256), 256)


def ring(me, axis):
    if axis == "x":
        return me.x, lambda step, dz=0: me.at(dx=step, dz=dz)
    return me.y, lambda step, dz=0: me.at(dy=step, dz=dz)


def add_rows(target, base, rows, cols, sources):
    step = min(rows.size, 64)

    @pl.loop(0, rows.size // step)
    def _(index):
        here = pl.ds(pl.multiple_of(index * step, step), step)
        there = pl.ds(pl.multiple_of(rows.start + index * step, 8), step)
        value = base[there, cols].astype(F32)
        for source in sources:
            value = value + source[here, :].astype(F32)
        target[there, cols] = value.astype(BF16)


def weight_sum(me, links, stages, parts, whole, slots, result, done_sem):
    row, rows, col, cols = 0, parts.shape[0], 0, parts.shape[1]
    pieces = []
    for index, ((kind, axis), slot) in enumerate(zip(stages, slots)):
        target = whole if index == len(stages) - 1 else parts
        across = pl.ds(col, cols)

        if kind == "pair":
            here = pl.ds(row, rows)
            cols = cols // 2
            own = pl.ds(pl.multiple_of(col + me.z * cols, 128), cols)
            other = pl.ds(pl.multiple_of(col + (1 - me.z) * cols, 128), cols)
            made = links.send(parts.at[here, other], slot, me.at(dz=1))
            pieces.append((here, own))
            yield
            made.wait_recv()
            add_rows(target, parts, here, own, [slot])
            col = own.start
            continue
        spot, to = ring(me, axis)
        if kind == "columns":
            here = pl.ds(row, rows)
            cols = cols // 8

            def strip(step, z, col=col, cols=cols, spot=spot):
                place = lax.rem(spot + step, 4) * 2 + z
                return pl.ds(pl.multiple_of(col + place * cols, 128), cols)

            pieces.append((here, strip))
            moves = []
            for step, dz in PLANE:
                piece = parts.at[here, strip(step, lax.rem(me.z + dz, 2))]
                moves.append(links.send(piece, slot.at[step * 2 + dz - 1], to(step, dz)))
            yield
            for made in moves:
                made.wait_recv()
            mine = strip(0, me.z)
            add_rows(target, parts, here, mine, [slot.at[index] for index in range(7)])
            continue
        rows = rows // (8 if kind == "plane" else 4)

        def chunk(step, z=None, row=row, rows=rows, spot=spot):
            place = lax.rem(spot + step, 4)
            place = place if z is None else place * 2 + z
            return pl.ds(pl.multiple_of(row + place * rows, 8), rows)

        pieces.append((chunk, across))
        if kind == "ring":
            low = pl.ds(col, cols // 2)
            high = pl.ds(col + cols // 2, cols // 2)
            first, second = pl.ds(0, cols // 2), pl.ds(cols // 2, cols // 2)
            side_up, side_down, main_up, main_down = slot
            far_up = links.send(parts.at[chunk(2), low], side_up, to(1))
            far_down = links.send(parts.at[chunk(2), high], side_down, to(3))
            near = [
                links.send(parts.at[chunk(1), high], main_up.at[:, second], to(1)),
                links.send(parts.at[chunk(3), low], main_down.at[:, first], to(3)),
            ]
            yield
            far_up.wait_recv()
            add_rows(parts, parts, chunk(1), low, [side_up])
            near.append(links.send(parts.at[chunk(1), low], main_up.at[:, first], to(1)))
            far_down.wait_recv()
            add_rows(parts, parts, chunk(3), high, [side_down])
            near.append(links.send(parts.at[chunk(3), high], main_down.at[:, second], to(3)))
            yield
            for made in near:
                made.wait_recv()
            add_rows(target, parts, chunk(0), across, [main_up, main_down])
            row = chunk(0).start
        elif kind == "direct":
            moves = [
                links.send(parts.at[chunk(step), across], slot.at[step - 1], to(step))
                for step in (1, 3, 2)
            ]
            yield
            for made in moves:
                made.wait_recv()
            add_rows(target, parts, chunk(0), across, [slot.at[step] for step in range(3)])
            row = chunk(0).start
        else:
            moves = []
            for step, dz in PLANE:
                piece = parts.at[chunk(step, lax.rem(me.z + dz, 2)), across]
                moves.append(links.send(piece, slot.at[step * 2 + dz - 1], to(step, dz)))
            yield
            for made in moves:
                made.wait_recv()
            mine = chunk(0, me.z)
            add_rows(target, parts, mine, across, [slot.at[index] for index in range(7)])
            row = mine.start
    for (kind, axis), (place, across) in zip(stages[::-1], pieces[::-1]):
        if kind == "pair":
            piece = whole.at[place, across]
            moves = [links.send(piece, piece, me.at(dz=1))]
            yield
        elif kind in ("plane", "columns"):
            _, to = ring(me, axis)
            piece = whole.at[place, across(0, me.z)] if kind == "columns" else whole.at[place(0, me.z), across]
            moves = [links.send(piece, piece, to(step, dz)) for step, dz in PLANE]
            yield
        elif kind == "direct":
            _, to = ring(me, axis)
            piece = whole.at[place(0), across]
            moves = [links.send(piece, piece, to(step)) for step in (1, 3, 2)]
            yield
        else:
            _, to = ring(me, axis)
            half = across.size // 2
            piece = whole.at[place(0), across]
            above = links.send(piece, piece, to(1))
            below = links.send(piece, piece, to(3))
            yield
            above.wait_recv()
            piece = whole.at[place(3), pl.ds(across.start, half)]
            moves = [links.send(piece, piece, to(1))]
            below.wait_recv()
            piece = whole.at[place(1), pl.ds(across.start + half, half)]
            moves.append(links.send(piece, piece, to(3)))
            yield
        for made in moves:
            made.wait_recv()
    copy = pltpu.make_async_copy(whole, result, done_sem)
    copy.start()
    yield
    copy.wait()


PLANE = [(1, 0), (3, 0), (0, 1), (1, 1), (3, 1), (2, 0), (2, 1)]


def vector_sum(me, links, values, plane, line, total):
    own = me.group
    plane[own] = values[...]
    here = plane.at[own]
    moves = [links.send(here, here, me.at(dy=step, dz=dz)) for step, dz in PLANE]
    yield
    for made in moves:
        made.wait_recv()
    value = plane[0]
    for slot in range(1, 8):
        value = value + plane[slot]
    line[me.x] = value
    here = line.at[me.x]
    moves = [links.send(here, here, me.at(dx=step)) for step in (1, 3, 2)]
    yield
    for made in moves:
        made.wait_recv()
    total[...] = line[0] + line[1] + line[2] + line[3]


def advance(jobs):
    for job in list(jobs):
        if next(job, "done") == "done":
            jobs.remove(job)


def list_mates(image_ref, next_of, mates, own):
    last = [jnp.int32(-1)] * 3
    for block in range(31, -1, -1):
        image = image_ref[block]
        next_of[block] = jnp.where(image == 0, last[0], jnp.where(image == 1, last[1], last[2]))
        last = [jnp.where(image == index, block, last[index]) for index in range(3)]
    for line in range(4):
        image = image_ref[line * 8 + own]
        first = jnp.where(image == 0, last[0], jnp.where(image == 1, last[1], last[2]))

        def list_one(index, block, line=line):
            known = jnp.maximum(block, 0)
            place = lax.rem(known, 8) * 4 + lax.div(known, 8)
            mates[line * 16 + index] = jnp.where(block < 0, -1, place)
            return jnp.where(block < 0, -1, next_of[known])

        lax.fori_loop(0, 16, list_one, first)


UP_STAGES = [("ring", "x"), ("direct", "y"), ("pair", None)]
DOWN_STAGES = [("ring", "y"), ("direct", "x"), ("pair", None)]
O_STAGES = [("direct", "x"), ("columns", "y")]
Q_STAGES = [("direct", "y"), ("plane", "x")]
K_STAGES = [("direct", "x"), ("plane", "y")]
V_STAGES = [("direct", "y"), ("plane", "x")]


def layer_kernel(
    x_hbm, cot_hbm, gain_one_ref, shift_one_ref, weight_hbm, attend_bias_ref, output_hbm,
    output_bias_ref, gain_two_ref, shift_two_ref, up_hbm, up_bias_ref, down_hbm, down_bias_ref,
    image_ref,
    result_out, input_out, vector_out, last_out, up_out, down_out, qkv_out, o_out,
    x_ref, cot_ref, weight_ref, up_ref, down_ref,
    first_low, kv, query_pair, kv_send, query_send, query_own, top, total, mixed,
    head_send, head_recv, attended, output_all, next_of, mates,
    hidden, xhat_two, inverse_two, second_low, down_grad, activated, pre_grad,
    branch_low, norm_parts, unit_parts, low_parts,
    grad_send, grad_pair, stats_all, grad_own, rows_all, query_grad_all,
    qg_send, qg_recv, kvg_send, kvg_recv, stacked,
    vector, plane_one, line_one, last, plane_two, line_two,
    job_up, job_down, job_q, job_k, job_v, job_o,
    send_sem, recv_sem, load_sem, done_sem,
):
    me = Place()
    links = Links(send_sem, recv_sem)
    at = me.high * 2 + me.core
    loads = []
    for source, target in (
        (x_hbm, x_ref), (weight_hbm, weight_ref), (output_hbm, output_all.at[at]), (up_hbm, up_ref),
        (down_hbm, down_ref), (cot_hbm, cot_ref),
    ):
        load = pltpu.make_async_copy(source, target, load_sem.at[len(loads)])
        load.start()
        loads.append(load)
    wait_all = greet(all_partners(me))
    own = me.group
    loads[0].wait()
    normed, _ = row_norm(x_ref[...])
    first_low[...] = (normed * gain_one_ref[...] + shift_one_ref[...]).astype(BF16)
    loads[1].wait()
    keys = dot_nn(first_low[...], weight_ref[1])
    values = dot_nn(first_low[...], weight_ref[2]) + attend_bias_ref[1:2, :]
    for head in range(4):
        part = slice(head * HEAD_DIM, (head + 1) * HEAD_DIM)
        kv_send[head] = jnp.concatenate([keys[:, part], values[:, part]], axis=1).astype(BF16)
    wait_all()
    kv_moves, query_moves = [], []
    for step in (1, 3, 2):
        head = lax.rem(me.x + step, 4)
        kv_moves.append(links.send(kv_send.at[head], kv.at[own * 4 + me.x], me.at(dx=step)))
    queries = dot_nn(first_low[...], weight_ref[0]) + attend_bias_ref[0:1, :]
    pack_heads(queries.astype(BF16).astype(F32) * (HEAD_DIM**-0.5), query_send)
    for step in (1, 3, 2):
        head = lax.rem(me.x + step, 4)
        query_moves.append(
            links.send(query_send.at[head], query_pair.at[own * 4 + me.x], me.at(dx=step))
        )
    kv[own * 4 + me.x] = kv_send[me.x]
    query_pair[own * 4 + me.x] = query_send[me.x]
    for made in kv_moves:
        made.wait_recv()
    gather = Gather(me, links, kv)
    gather.begin()
    top[...] = jnp.full(top.shape, LOWEST, F32)
    total[...] = jnp.zeros(total.shape, F32)
    mixed[...] = jnp.zeros(mixed.shape, F32)
    list_mates(image_ref, next_of, mates, own)
    for made in query_moves:
        made.wait_recv()
    for block in range(4):
        pair = query_pair[own * 4 + block].astype(F32)
        both = jnp.concatenate([pair, pltpu.roll(pair, 64, 1)], axis=0)
        query_own[block] = jnp.where(lanes_below(both.shape), both, 0.0).astype(BF16)

    def attend(slot):
        keys = [kv[slot * 4 + part] for part in range(4)]
        images = [image_ref[part * 8 + slot] for part in range(4)]
        scores = [[dot_nt(query_own[block], key) for key in keys] for block in range(4)]
        joined = jnp.concatenate(keys, axis=0)
        state = []
        for block in range(4):
            mine = image_ref[block * 8 + own]
            highest, shut = None, []
            for part in range(4):
                same = images[part] == mine
                shut.append(jnp.where(same, -3e38, HIGHEST))
                score = scores[block][part]
                peak = jnp.maximum(score[:, :128], score[:, 128:])
                peak = jnp.minimum(peak, jnp.where(same, 3e38, LOWEST))
                highest = peak if highest is None else jnp.maximum(highest, peak)
            before = top[block]
            now = jnp.maximum(before, spread(jnp.max(highest, axis=1, keepdims=True)))
            top[block] = now
            state.append((now, jnp.exp(before - now), shut))
        for block, (now, fade, shut) in enumerate(state):
            sums = total[block] * fade
            probs = []
            for part in range(4):
                level = jnp.maximum(now, shut[part])
                prob = jnp.exp(scores[block][part] - wide(level))
                sums = sums + prob[:, :128] + prob[:, 128:]
                probs.append(prob.astype(BF16))
            total[block] = sums
            mixed[block] = mixed[block] * fade + dot_nn(jnp.concatenate(probs, axis=1), joined)

    def attend_near(z):
        @pl.loop(0, 2)
        def _(side):
            attend(gather.slot(3 - 2 * side, z))

    attend(own)
    gather.pass_z()
    attend(gather.slot(0, gather.other))
    gather.pass_own()
    attend_near(me.z)
    gather.pass_other()
    gather.end_near()
    attend_near(gather.other)
    gather.end_own()
    loads[2].wait()
    quarter = pl.ds(pl.multiple_of(me.x * 64, 64), 64)
    piece = output_all.at[at, quarter]
    output_high = links.send(piece, piece, me.at(dhigh=1))
    output_core = links.send(output_all.at[at], output_all.at[at], me.at(dcore=1))
    attend(gather.slot(2, me.z))
    gather.end_other()
    across = (1 - me.high) * 2 + me.core
    output_high.wait_recv()
    piece = output_all.at[across, quarter]
    output_moves = [links.send(piece, piece, me.at(dx=step)) for step in (1, 3, 2)]
    query_gather = Gather(me, links, query_pair)
    query_gather.begin()
    attend(gather.slot(2, gather.other))
    for block in range(4):
        sums = spread(jnp.sum(total[block], axis=1, keepdims=True))
        out = mixed[block] / sums
        mixed[block] = out
        top[block] = top[block] + jnp.log(sums)
        back = pltpu.roll(out[:128, :], 64, 1)
        head_send[block] = jnp.where(lanes_below(back.shape), back, out[128:, :]).astype(BF16)
    head_moves = []
    for step in (1, 3, 2):
        to = lax.rem(me.x + step, 4)
        head_moves.append(links.send(head_send.at[to], head_recv.at[me.x], me.at(dx=step)))
    head_recv[me.x] = head_send[me.x]
    for made in output_moves:
        made.wait_recv()
    output_pass = links.send(output_all.at[across], output_all.at[across], me.at(dcore=1))
    for block in range(4):
        stats_all[own, block : block + 1, :] = top[block].T[0:1, :]
    for made in head_moves:
        made.wait_recv()
    attended[at] = unpack_heads(head_recv)
    here = attended.at[at]
    attended_high = links.send(here, here, me.at(dhigh=1))
    attended_core = links.send(here, here, me.at(dcore=1))
    query_gather.pass_z()
    query_gather.pass_own()
    output_core.wait_recv()
    output_pass.wait_recv()
    attended_high.wait_recv()
    attended_pass = links.send(attended.at[across], attended.at[across], me.at(dcore=1))
    query_gather.pass_other()
    attended_core.wait_recv()
    attended_pass.wait_recv()

    @pl.loop(0, 4)
    def _(step):
        cols = cols_of(step)
        value = x_ref[:, cols] + output_bias_ref[:, cols]
        for part in range(4):
            value = value + dot_nn(attended[part], output_all[part, :, cols])
        hidden[:, cols] = value

    normed, inverse = row_norm(hidden[...])
    xhat_two[...] = normed
    inverse_two[...] = spread(inverse)
    second_low[...] = (normed * gain_two_ref[...] + shift_two_ref[...]).astype(BF16)
    loads[5].wait()
    down_grad[...] = cot_ref[...].astype(BF16)
    loads[3].wait()
    loads[4].wait()

    @pl.loop(0, 4)
    def _(step):
        cols = cols_of(step)
        pre = dot_nn(second_low[...], up_ref[:, cols]) + up_bias_ref[:, cols]
        back = dot_nt(down_grad[...], down_ref[cols, :])
        chance = 0.5 + 0.5 * lax.erf(pre * (0.5**0.5))
        density = jnp.exp(-0.5 * pre * pre) * 0.3989422804014327
        activated[:, cols] = (pre * chance).astype(BF16)
        low = (back * (chance + pre * density)).astype(BF16)
        pre_grad[:, cols] = low
        vector[4:5, cols] = jnp.sum(low.astype(F32), axis=0, keepdims=True)

    norm_sum = ModelSum(me, links, *norm_parts)
    norm_sum.begin(lambda cols: dot_nt(pre_grad[...], up_ref[cols, :]))

    @pl.loop(0, 4)
    def _(step):
        cols = cols_of(step)
        job_down[0][cols, :] = dot_tn(activated[:, cols], down_grad[...]).astype(BF16)

    downs = [weight_sum(me, links, DOWN_STAGES, *job_down, down_out, done_sem.at[1])]
    norm_sum.cross()
    query_gather.end_near()
    query_gather.end_own()
    query_gather.end_other()
    advance(downs)

    @pl.loop(0, 4)
    def _(step):
        cols = cols_of(step)
        job_up[0][cols, :] = dot_tn(second_low[:, cols], pre_grad[...]).astype(BF16)

    ups = [weight_sum(me, links, UP_STAGES, *job_up, up_out, done_sem.at[0])]
    advance(ups)
    unit_sum = ModelSum(me, links, *unit_parts)
    unit_sum.begin(lambda cols: dot_nn(activated[...], down_ref[:, cols]))
    vector[3:4, :] = jnp.sum(down_grad[...].astype(F32), axis=0, keepdims=True)
    advance(downs)
    norm_sum.back()
    norm_sum.end()
    grad = norm_sum.full[...].astype(F32)
    xhat = xhat_two[...]
    vector[0:1, :] = jnp.sum(grad * xhat, axis=0, keepdims=True)
    vector[1:2, :] = jnp.sum(grad, axis=0, keepdims=True)
    scaled = grad * gain_two_ref[...]
    hidden_grad = cot_ref[...] + (
        scaled
        - jnp.mean(scaled, axis=-1, keepdims=True)
        - xhat * jnp.mean(scaled * xhat, axis=-1, keepdims=True)
    ) * inverse_two[:, 0:1]
    cot_ref[...] = hidden_grad
    low = hidden_grad.astype(BF16)
    branch_low[...] = low
    vector[2:3, :] = jnp.sum(low.astype(F32), axis=0, keepdims=True)
    pack_heads(dot_nt(branch_low[...], output_all[at]).astype(BF16).astype(F32), grad_send)
    moves = []
    for step in (1, 3, 2):
        head = lax.rem(me.x + step, 4)
        moves.append(links.send(grad_send.at[head], grad_pair.at[own * 4 + me.x], me.at(dx=step)))
    grad_pair[own * 4 + me.x] = grad_send[me.x]
    advance(ups)

    @pl.loop(0, 4)
    def _(step):
        cols = cols_of(step)
        job_o[0][:, cols] = dot_tn(attended[at], branch_low[:, cols]).astype(BF16)

    for made in moves:
        made.wait_recv()
    gather = Gather(me, links, grad_pair)
    gather.begin()

    @pl.loop(0, 4)
    def _(block):
        pair = grad_pair[own * 4 + block].astype(F32)
        both = jnp.concatenate([pltpu.roll(pair, 64, 1), pair], axis=0)
        both = jnp.where(lanes_below(both.shape), 0.0, both)
        grad_own[block] = both.astype(BF16)
        delta = spread(jnp.sum(both * mixed[block], axis=1, keepdims=True))
        total[block] = delta
        stats_all[own, pl.ds(block + 4, 1), :] = delta.T[0:1, :]

    here = stats_all.at[own]
    stats_moves = [links.send(here, here, me.at(dy=step, dz=dz)) for step, dz in PLANE]

    def query_pass(block):
        query, grad_out = query_own[block], grad_own[block]
        level, delta = top[block], wide(total[block])

        def some(step, acc):
            keys, changes = [], []
            for part in range(8):
                place = mates[block * 16 + step * 8 + part]
                key = kv[jnp.maximum(place, 0)]
                shut = jnp.where(place < 0, HIGHEST, -3e38)
                prob = jnp.exp(dot_nt(query, key) - wide(jnp.maximum(level, shut)))
                changes.append((prob * (dot_nt(grad_out, key) - delta)).astype(BF16))
                keys.append(key)
            return acc + dot_nn(jnp.concatenate(changes, axis=1), jnp.concatenate(keys, axis=0))

        acc = lax.fori_loop(0, 2, some, jnp.zeros((256, 128), F32))
        qg_send[block] = pack_rows(acc * (HEAD_DIM**-0.5)).astype(BF16)

    query_moves = []

    def send_query(step):
        block = lax.rem(me.x + step, 4)
        query_pass(block)
        if step:
            query_moves.append(links.send(qg_send.at[block], qg_recv.at[me.x], me.at(dx=step)))
        else:
            qg_recv[me.x] = qg_send[me.x]

    def pair_up(slot):
        @pl.loop(0, 4)
        def _(block):
            spot = slot * 4 + block
            pair = query_pair[spot].astype(F32)
            other = grad_pair[spot].astype(F32)
            keep = lanes_below(pair.shape)
            upper = jnp.where(keep, pair, pltpu.roll(other, 64, 1))
            lower = jnp.where(keep, pltpu.roll(pair, 64, 1), other)
            query_grad_all[spot] = jnp.concatenate([upper, lower], axis=0).astype(BF16)
            rows_all[spot, 0:1, :] = stats_all[slot, pl.ds(block, 1), :]
            rows_all[spot, 1:2, :] = stats_all[slot, pl.ds(block + 4, 1), :]

    send_query(2)
    gather.pass_z()
    advance(downs)
    send_query(1)
    gather.pass_own()
    outs = [weight_sum(me, links, O_STAGES, *job_o, o_out, done_sem.at[5])]
    advance(outs)
    advance(ups)
    for made in stats_moves:
        made.wait_recv()
    pair_up(own)
    pair_up(gather.slot(0, gather.other))
    send_query(3)
    gather.pass_other()
    pair_up(gather.slot(1, me.z))
    pair_up(gather.slot(3, me.z))
    send_query(0)
    gather.end_own()
    advance(downs)
    gather.end_near()
    pair_up(gather.slot(2, me.z))
    pair_up(gather.slot(1, gather.other))
    pair_up(gather.slot(3, gather.other))
    gather.end_other()
    pair_up(gather.slot(2, gather.other))
    advance(ups)
    advance(downs)
    advance(outs)

    def key_pass(block):
        both = kv[own * 4 + block].astype(F32)
        keep = lanes_below(both.shape)
        key = jnp.where(keep, both, 0.0).astype(BF16)
        value = jnp.where(keep, 0.0, both).astype(BF16)

        def some(step, accs):
            pairs, probs, changes = [], [], []
            for part in range(8):
                place = mates[block * 16 + step * 8 + part]
                spot = jnp.maximum(place, 0)
                shut = jnp.where(place < 0, HIGHEST, -3e38)
                pair, lines = query_grad_all[spot], rows_all[spot]
                prob = jnp.exp(dot_nt(key, pair) - jnp.maximum(lines[0:1, :], shut))
                probs.append(prob.astype(BF16))
                changes.append((prob * (dot_nt(value, pair) - lines[1:2, :])).astype(BF16))
                pairs.append(pair)
            joined = jnp.concatenate(pairs, axis=0)
            return (
                accs[0] + dot_nn(jnp.concatenate(changes, axis=1), joined),
                accs[1] + dot_nn(jnp.concatenate(probs, axis=1), joined),
            )

        zero = jnp.zeros((256, 128), F32)
        of_key, of_value = lax.fori_loop(0, 2, some, (zero, zero))
        kvg_send[block] = jnp.where(keep, of_key, of_value).astype(BF16)

    key_moves = []

    def send_key(step):
        block = lax.rem(me.x + step, 4)
        key_pass(block)
        if step:
            key_moves.append(links.send(kvg_send.at[block], kvg_recv.at[me.x], me.at(dx=step)))
        else:
            kvg_recv[me.x] = kvg_send[me.x]

    send_key(2)
    advance(ups)
    for made in query_moves:
        made.wait_recv()
    stacked[:, 0:256] = unpack_heads(qg_recv)
    job_q[0][...] = dot_tn(first_low[...], stacked[:, 0:256]).astype(BF16)
    jobs = [weight_sum(me, links, Q_STAGES, *job_q, qkv_out.at[0], done_sem.at[2])]
    advance(jobs)
    advance(outs)
    send_key(1)
    advance(downs)
    send_key(3)
    advance(ups)
    send_key(0)
    advance(jobs)
    advance(outs)
    for made in key_moves:
        made.wait_recv()

    heads = [kvg_recv[head].astype(F32) for head in range(4)]
    stacked[:, 256:512] = jnp.concatenate([value[:, :64] for value in heads], axis=1).astype(BF16)
    stacked[:, 512:768] = jnp.concatenate([value[:, 64:] for value in heads], axis=1).astype(BF16)
    low_sum = ModelSum(me, links, *low_parts)
    low_sum.begin(
        lambda cols: dot_nt(stacked[:, 0:256], weight_ref[0, cols, :])
        + dot_nt(stacked[:, 256:512], weight_ref[1, cols, :])
        + dot_nt(stacked[:, 512:768], weight_ref[2, cols, :])
    )
    job_k[0][...] = dot_tn(first_low[...], stacked[:, 256:512]).astype(BF16)
    job_v[0][...] = dot_tn(first_low[...], stacked[:, 512:768]).astype(BF16)
    pairs = [
        weight_sum(me, links, K_STAGES, *job_k, qkv_out.at[1], done_sem.at[3]),
        weight_sum(me, links, V_STAGES, *job_v, qkv_out.at[2], done_sem.at[4]),
    ]
    advance(pairs)
    low_sum.cross()
    unit_sum.cross()
    vector[5:6, 0:256] = jnp.sum(stacked[:, 0:256].astype(F32), axis=0, keepdims=True)
    vector[5:6, 256:512] = jnp.sum(stacked[:, 512:768].astype(F32), axis=0, keepdims=True)
    vector[5:6, 512:1024] = jnp.zeros((1, 512), F32)
    vector[6:8, :] = jnp.zeros((2, 1024), F32)
    vectors = [vector_sum(me, links, vector, plane_one, line_one, vector_out)]
    advance(vectors)
    advance(jobs)
    advance(downs)
    advance(ups)
    xhat, inverse = row_norm(x_ref[...])
    low_sum.back()
    advance(pairs)
    low_sum.end()
    grad = low_sum.full[...].astype(F32)
    gain_grad = jnp.sum(grad * xhat, axis=0, keepdims=True)
    shift_grad = jnp.sum(grad, axis=0, keepdims=True)
    for part in range(4):
        cols = slice(part * 256, (part + 1) * 256)
        last[part : part + 1, :] = gain_grad[:, cols]
        last[part + 4 : part + 5, :] = shift_grad[:, cols]
    vectors.append(vector_sum(me, links, last, plane_two, line_two, last_out))
    advance(vectors)
    scaled = grad * gain_one_ref[...]
    cot_ref[...] = cot_ref[...] + (
        scaled
        - jnp.mean(scaled, axis=-1, keepdims=True)
        - xhat * jnp.mean(scaled * xhat, axis=-1, keepdims=True)
    ) * inverse
    input_done = pltpu.make_async_copy(cot_ref, input_out, done_sem.at[6])
    input_done.start()
    unit_sum.back()
    unit_sum.end()
    hidden[...] = hidden[...] + unit_sum.full[...].astype(F32) + down_bias_ref[...]
    result_done = pltpu.make_async_copy(hidden, result_out, done_sem.at[7])
    result_done.start()
    jobs = pairs + vectors + jobs + ups + downs + outs
    while jobs:
        advance(jobs)
    input_done.wait()
    result_done.wait()
    links.finish()


def job_scratch(height, width, stages):
    slots = []
    rows, cols = height, width
    for kind, _ in stages:
        if kind == "ring":
            rows = rows // 4
            side, main = pltpu.VMEM((rows, cols // 2), BF16), pltpu.VMEM((rows, cols), BF16)
            slots.append([side, side, main, main])
        elif kind == "direct":
            rows = rows // 4
            slots.append(pltpu.VMEM((3, rows, cols), BF16))
        elif kind == "plane":
            rows = rows // 8
            slots.append(pltpu.VMEM((7, rows, cols), BF16))
        elif kind == "columns":
            cols = cols // 8
            slots.append(pltpu.VMEM((7, rows, cols), BF16))
        else:
            cols = cols // 2
            slots.append(pltpu.VMEM((rows, cols), BF16))
    return [pltpu.VMEM((height, width), BF16), pltpu.VMEM((height, width), BF16), slots]


def sum_scratch():
    half = pltpu.VMEM((128, 1024), BF16)
    whole = pltpu.VMEM((256, 1024), BF16)
    return [whole, half, half, half, whole]


def layer(*args):
    vmem = pl.BlockSpec(memory_space=pltpu.VMEM)
    smem = pl.BlockSpec(memory_space=pltpu.SMEM)
    hbm = pl.BlockSpec(memory_space=pl.ANY)
    low_rows = pltpu.VMEM((256, 1024), BF16)
    wide_rows = pltpu.VMEM((256, 1024), F32)
    return pl.pallas_call(
        layer_kernel,
        out_shape=[
            jax.ShapeDtypeStruct((256, 1024), F32),
            jax.ShapeDtypeStruct((256, 1024), F32),
            jax.ShapeDtypeStruct((8, 1024), F32),
            jax.ShapeDtypeStruct((8, 256), F32),
            jax.ShapeDtypeStruct((1024, 1024), BF16),
            jax.ShapeDtypeStruct((1024, 1024), BF16),
            jax.ShapeDtypeStruct((3, 1024, 256), BF16),
            jax.ShapeDtypeStruct((256, 1024), BF16),
        ],
        in_specs=[hbm, hbm, vmem, vmem, hbm, vmem, hbm, vmem, vmem, vmem, hbm, vmem, hbm, vmem, smem],
        out_specs=[hbm] * 2 + [vmem] * 2 + [hbm] * 4,
        scratch_shapes=[
            wide_rows, wide_rows,
            pltpu.VMEM((3, 1024, 256), BF16),
            pltpu.VMEM((1024, 1024), BF16), pltpu.VMEM((1024, 1024), BF16),
            low_rows,
            pltpu.VMEM((32, 256, 128), BF16),
            pltpu.VMEM((32, 128, 128), BF16),
            pltpu.VMEM((4, 256, 128), BF16),
            pltpu.VMEM((4, 128, 128), BF16),
            pltpu.VMEM((4, 256, 128), BF16),
            pltpu.VMEM((4, 256, 128), F32),
            pltpu.VMEM((4, 256, 128), F32),
            pltpu.VMEM((4, 256, 128), F32),
            pltpu.VMEM((4, 128, 128), BF16),
            pltpu.VMEM((4, 128, 128), BF16),
            pltpu.VMEM((4, 256, 256), BF16),
            pltpu.VMEM((4, 256, 1024), BF16),
            pltpu.SMEM((32,), jnp.int32),
            pltpu.SMEM((64,), jnp.int32),
            wide_rows, wide_rows, pltpu.VMEM((256, 128), F32),
            low_rows, low_rows, low_rows, low_rows, low_rows,
            sum_scratch(), sum_scratch(), sum_scratch(),
            pltpu.VMEM((4, 128, 128), BF16),
            pltpu.VMEM((32, 128, 128), BF16),
            pltpu.VMEM((8, 8, 256), F32),
            pltpu.VMEM((4, 256, 128), BF16),
            pltpu.VMEM((32, 8, 256), F32),
            pltpu.VMEM((32, 256, 128), BF16),
            pltpu.VMEM((4, 128, 128), BF16),
            pltpu.VMEM((4, 128, 128), BF16),
            pltpu.VMEM((4, 256, 128), BF16),
            pltpu.VMEM((4, 256, 128), BF16),
            pltpu.VMEM((256, 768), BF16),
            pltpu.VMEM((8, 1024), F32), pltpu.VMEM((8, 8, 1024), F32), pltpu.VMEM((4, 8, 1024), F32),
            pltpu.VMEM((8, 256), F32), pltpu.VMEM((8, 8, 256), F32), pltpu.VMEM((4, 8, 256), F32),
            job_scratch(1024, 1024, UP_STAGES),
            job_scratch(1024, 1024, DOWN_STAGES),
            job_scratch(1024, 256, Q_STAGES),
            job_scratch(1024, 256, K_STAGES),
            job_scratch(1024, 256, V_STAGES),
            job_scratch(256, 1024, O_STAGES),
            pltpu.SemaphoreType.DMA((240,)),
            pltpu.SemaphoreType.DMA((240,)),
            pltpu.SemaphoreType.DMA((6,)),
            pltpu.SemaphoreType.DMA((8,)),
        ],
        compiler_params=pltpu.CompilerParams(
            collective_id=0, has_side_effects=True, vmem_limit_bytes=VMEM_BYTES
        ),
    )(*args)


def widen_kernel(
    up, down, qkv, o, result, input_grad, vector, last,
    up_out, down_out, qkv_out, o_out, result_out, input_out,
    first_gain, first_shift, bias, output_bias, second_gain, second_shift, up_bias, down_bias,
):
    up_out[...] = up[...].astype(F32)
    down_out[...] = down[...].astype(F32)
    qkv_out[...] = qkv[...].astype(F32)
    o_out[...] = o[...].astype(F32)
    result_out[...] = result[...]
    input_out[...] = input_grad[...]

    @pl.when(pl.program_id(0) == 0)
    def _():
        first_gain[...] = jnp.concatenate([last[row : row + 1, :] for row in range(4)], axis=1)
        first_shift[...] = jnp.concatenate([last[row : row + 1, :] for row in range(4, 8)], axis=1)
        bias[0:1, :] = vector[5:6, 0:256]
        bias[1:2, :] = vector[5:6, 256:512]
        for target, row in (
            (second_gain, 0), (second_shift, 1), (output_bias, 2), (down_bias, 3), (up_bias, 4),
        ):
            target[...] = vector[row : row + 1, :]


def widen(up, down, qkv, o, result, input_grad, vector, last):
    steps = 8
    tall = pl.BlockSpec((1024 // steps, 1024), lambda step: (step, 0))
    short = pl.BlockSpec((256 // steps, 1024), lambda step: (step, 0))
    three = pl.BlockSpec((3, 1024 // steps, 256), lambda step: (0, step, 0))
    line = pl.BlockSpec((1, 1024), lambda step: (0, 0))

    def whole(shape):
        return pl.BlockSpec(shape, lambda step: (0, 0))

    row = jax.ShapeDtypeStruct((1, 1024), F32)
    return pl.pallas_call(
        widen_kernel,
        grid=(steps,),
        out_shape=[
            jax.ShapeDtypeStruct((1024, 1024), F32),
            jax.ShapeDtypeStruct((1024, 1024), F32),
            jax.ShapeDtypeStruct((3, 1024, 256), F32),
            jax.ShapeDtypeStruct((256, 1024), F32),
            jax.ShapeDtypeStruct((256, 1024), F32),
            jax.ShapeDtypeStruct((256, 1024), F32),
            row, row, jax.ShapeDtypeStruct((2, 256), F32), row, row, row, row, row,
        ],
        in_specs=[tall, tall, three, short, short, short, whole((8, 1024)), whole((8, 256))],
        out_specs=[
            tall, tall, three, short, short, short,
            line, line, whole((2, 256)), line, line, line, line, line,
        ],
        compiler_params=pltpu.CompilerParams(vmem_limit_bytes=VMEM_BYTES),
    )(up, down, qkv, o, result, input_grad, vector, last)


def per_device(
    inputs,
    first_gain,
    first_shift,
    attend_weight,
    attend_bias,
    output_weight,
    output_bias,
    second_gain,
    second_shift,
    up_weight,
    up_bias,
    down_weight,
    down_bias,
    image_of,
    cotangent,
):
    result, input_grad, vector, last, up, down, qkv, o = layer(
        inputs, cotangent, first_gain[None], first_shift[None], attend_weight, attend_bias,
        output_weight, output_bias[None], second_gain[None], second_shift[None],
        up_weight, up_bias[None], down_weight, down_bias[None], image_of,
    )
    (
        up, down, qkv, o, result, input_grad, first_gain_grad, first_shift_grad, bias_grad,
        output_bias_grad, second_gain_grad, second_shift_grad, up_bias_grad, down_bias_grad,
    ) = widen(up, down, qkv, o, result, input_grad, vector, last)
    return (
        result, input_grad, first_gain_grad[0], first_shift_grad[0], qkv, bias_grad, o,
        output_bias_grad[0], second_gain_grad[0], second_shift_grad[0], up, up_bias_grad[0], down,
        down_bias_grad[0],
    )


def solution(mesh):
    in_specs = (
        P("dp", None), P(), P(), P(None, None, "mp"), P(None, "mp"), P("mp", None), P(), P(), P(),
        P(None, "mp"), P("mp"), P("mp", None), P(), P(), P("dp", None),
    )
    out_specs = (
        P("dp", None), P("dp", None), P(), P(), P(None, None, "mp"), P(None, "mp"), P("mp", None),
        P(), P(), P(), P(None, "mp"), P("mp"), P("mp", None), P(),
    )
    return jax.shard_map(
        per_device, mesh=mesh, in_specs=in_specs, out_specs=out_specs, check_vma=False
    )
```

```python
import functools

import jax
import jax.numpy as jnp
from jax import lax
from jax.experimental import pallas as pl
from jax.experimental.pallas import tpu as pltpu
from jax.sharding import PartitionSpec as P

HEAD_DIM = 64
EPSILON = 1e-06
LOWEST = -1e30
HIGHEST = 1e30
MESH = pl.DeviceIdType.MESH
F32 = jnp.float32
BF16 = jnp.bfloat16
VMEM_BYTES = 60 * 2**20


def dot_nn(left, right):
    return lax.dot_general(left, right, (((1,), (0,)), ((), ())), preferred_element_type=F32)


def dot_nt(left, right):
    return lax.dot_general(left, right, (((1,), (1,)), ((), ())), preferred_element_type=F32)


def dot_tn(left, right):
    return lax.dot_general(left, right, (((0,), (0,)), ((), ())), preferred_element_type=F32)


class Place:
    def __init__(self):
        data, model = lax.axis_index("dp"), lax.axis_index("mp")
        self.x = lax.div(data, 8)
        self.y = lax.rem(lax.div(data, 2), 4)
        self.z = lax.rem(data, 2)
        self.high = lax.div(model, 2)
        self.core = lax.rem(model, 2)
        self.group = self.y * 2 + self.z

    def at(self, dx=0, dy=0, dz=0, dhigh=0, dcore=0):
        x = lax.rem(self.x + dx, 4)
        y = lax.rem(self.y + dy, 4)
        z = lax.rem(self.z + dz, 2)
        high = lax.rem(self.high + dhigh, 2)
        core = lax.rem(self.core + dcore, 2)
        return (x * 8 + y * 2 + z, high * 2 + core)


class Links:
    def __init__(self, send_sem, recv_sem):
        self.send_sem, self.recv_sem = send_sem, recv_sem
        self.used = 0
        self.sent = []

    def copy(self, source, target, device):
        at = self.used
        self.used += 1
        made = pltpu.make_async_remote_copy(
            src_ref=source,
            dst_ref=target,
            send_sem=self.send_sem.at[at],
            recv_sem=self.recv_sem.at[at],
            device_id=device,
            device_id_type=MESH,
        )
        self.sent.append(made)
        return made

    def send(self, source, target, device):
        made = self.copy(source, target, device)
        made.start()
        return made

    def finish(self):
        for made in self.sent:
            made.wait_send()
        self.sent = []


def greet(partners):
    barrier = pltpu.get_barrier_semaphore()
    for device in partners:
        pl.semaphore_signal(barrier, inc=1, device_id=device, device_id_type=MESH)
    return lambda: pl.semaphore_wait(barrier, len(partners))


def all_partners(me):
    near = [me.at(dx=step) for step in (1, 2, 3)]
    near += [me.at(dx=step, dz=1) for step in (1, 2, 3)]
    near += [me.at(dy=step) for step in (1, 2, 3)]
    near += [me.at(dy=step, dz=1) for step in (1, 2, 3)]
    near += [me.at(dx=step, dhigh=1) for step in (1, 2, 3)]
    return near + [me.at(dz=1), me.at(dhigh=1), me.at(dcore=1)]


def row_norm(values):
    mean = jnp.mean(values, axis=-1, keepdims=True)
    centred = values - mean
    variance = jnp.mean(centred * centred, axis=-1, keepdims=True)
    inverse = lax.rsqrt(variance + EPSILON)
    return centred * inverse, inverse


def spread(column):
    return jnp.broadcast_to(column, (column.shape[0], 128))


def wide(value):
    return jnp.concatenate([value, value], axis=1)


def lanes_below(shape):
    return lax.broadcasted_iota(jnp.int32, shape, 1) < HEAD_DIM


def pack_rows(values):
    return jnp.where(lanes_below((128, 128)), values[:128, :], pltpu.roll(values[128:, :], 64, 1))


def pack_heads(values, target):
    for head in range(4):
        part = slice(head * HEAD_DIM, (head + 1) * HEAD_DIM)
        target[head] = jnp.concatenate([values[:128, part], values[128:, part]], axis=1).astype(BF16)


def unpack_heads(source):
    heads = [source[head].astype(F32) for head in range(4)]
    upper = jnp.concatenate([value[:, :HEAD_DIM] for value in heads], axis=1)
    lower = jnp.concatenate([value[:, HEAD_DIM:] for value in heads], axis=1)
    return jnp.concatenate([upper, lower], axis=0).astype(BF16)


class Gather:
    def __init__(self, me, links, blocks):
        self.me, self.links, self.blocks = me, links, blocks
        self.other = 1 - me.z

    def slot(self, dy, z):
        return lax.rem(self.me.y + dy, 4) * 2 + z

    def send(self, slot, first, count, device):
        piece = self.blocks.at[pl.ds(slot * 4 + first, count)]
        return self.links.send(piece, piece, device)

    def begin(self):
        me = self.me
        self.up, self.down, self.across = me.at(dy=1), me.at(dy=3), me.at(dz=1)
        own = me.group
        self.own_y = [self.send(own, 0, 4, self.up), self.send(own, 0, 4, self.down)]
        self.from_z = self.send(own, 0, 4, self.across)

    def pass_z(self):
        self.from_z.wait_recv()
        slot = self.slot(0, self.other)
        self.other_y = [self.send(slot, 0, 2, self.up), self.send(slot, 0, 2, self.down)]

    def pass_own(self):
        below, above = self.slot(3, self.me.z), self.slot(1, self.me.z)
        self.own_y[0].wait_recv()
        self.far_own = [self.send(below, 0, 2, self.up)]
        self.rest = [self.send(below, 2, 2, self.across)]
        self.own_y[1].wait_recv()
        self.far_own.append(self.send(above, 2, 2, self.down))
        self.rest.append(self.send(above, 2, 2, self.across))

    def pass_other(self):
        below, above = self.slot(3, self.other), self.slot(1, self.other)
        self.other_y[0].wait_recv()
        self.far_other = [self.send(below, 0, 1, self.up)]
        self.other_y[1].wait_recv()
        self.far_other.append(self.send(above, 1, 1, self.down))

    def end_near(self):
        for made in self.rest:
            made.wait_recv()

    def end_own(self):
        self.far_own[1].wait_recv()
        self.last = self.send(self.slot(2, self.me.z), 2, 2, self.across)
        self.far_own[0].wait_recv()

    def end_other(self):
        for made in self.far_other + [self.last]:
            made.wait_recv()


class ModelSum:
    def __init__(self, me, links, part, pair, half, far, full):
        self.me, self.links = me, links
        self.part, self.pair, self.half, self.far, self.full = part, pair, half, far, full
        self.own = pl.ds(pl.multiple_of(me.core * 128, 128), 128)
        self.other = pl.ds(pl.multiple_of((1 - me.core) * 128, 128), 128)

    def cols(self, side):
        return pl.ds(side * 512, 512)

    def begin(self, tile):
        self.first, self.second, self.third = [], [], []
        for side in range(2):

            @pl.loop(2 * side, 2 * side + 2)
            def _(step):
                cols = cols_of(step)
                self.part[:, cols] = tile(cols).astype(BF16)

            cols = self.cols(side)
            self.first.append(
                self.links.send(
                    self.part.at[self.other, cols], self.pair.at[:, cols], self.me.at(dcore=1)
                )
            )

    def cross(self, side):
        cols = self.cols(side)
        self.first[side].wait_recv()
        value = self.part[self.own, cols].astype(F32) + self.pair[:, cols].astype(F32)
        self.half[:, cols] = value.astype(BF16)
        self.second.append(
            self.links.send(self.half.at[:, cols], self.far.at[:, cols], self.me.at(dhigh=1))
        )

    def back(self):
        for side in range(2):
            cols = self.cols(side)
            self.second[side].wait_recv()
            value = self.half[:, cols].astype(F32) + self.far[:, cols].astype(F32)
            self.full[self.own, cols] = value.astype(BF16)
            piece = self.full.at[self.own, cols]
            self.third.append(self.links.send(piece, piece, self.me.at(dcore=1)))

    def end(self):
        for made in self.third:
            made.wait_recv()


def cols_of(step):
    return pl.ds(pl.multiple_of(step * 256, 256), 256)


def ring(me, axis):
    if axis == "x":
        return me.x, lambda step, dz=0: me.at(dx=step, dz=dz)
    return me.y, lambda step, dz=0: me.at(dy=step, dz=dz)


def add_rows(target, base, rows, cols, sources, shift=0):
    step = min(rows.size, 64)

    @pl.loop(0, rows.size // step)
    def _(index):
        here = pl.ds(pl.multiple_of(index * step, step), step)
        there = pl.ds(pl.multiple_of(rows.start + index * step, 8), step)
        value = base[there, cols].astype(F32)
        for source in sources:
            value = value + source[here, :].astype(F32)
        there = pl.ds(pl.multiple_of(rows.start + shift + index * step, 8), step)
        target[there, cols] = value.astype(BF16)


def weight_sum(me, links, stages, parts, whole, slots, result, done_sem):
    row, rows, col, cols = 0, parts.shape[0], 0, parts.shape[1]
    pieces = []
    shift = 0

    def moved(place):
        return pl.ds(pl.multiple_of(place.start + shift, 8), place.size)

    for index, ((kind, axis), slot) in enumerate(zip(stages, slots)):
        target, add = (whole, shift) if index == len(stages) - 1 else (parts, 0)
        across = pl.ds(col, cols)
        if kind == "summed":
            spot, to = ring(me, axis)
            shift = spot * rows

            def chunk(step, rows=rows, spot=spot):
                return pl.ds(lax.rem(spot + step, 4) * rows - spot * rows, rows)

            pieces.append((chunk, across))
            continue

        if kind == "pair":
            here = pl.ds(row, rows)
            cols = cols // 2
            own = pl.ds(pl.multiple_of(col + me.z * cols, 128), cols)
            other = pl.ds(pl.multiple_of(col + (1 - me.z) * cols, 128), cols)
            made = links.send(parts.at[here, other], slot, me.at(dz=1))
            pieces.append((moved(here), own))
            yield
            made.wait_recv()
            add_rows(target, parts, here, own, [slot], add)
            col = own.start
            continue
        spot, to = ring(me, axis)
        if kind == "columns":
            here = pl.ds(row, rows)
            cols = cols // 8

            def strip(step, z, col=col, cols=cols, spot=spot):
                place = lax.rem(spot + step, 4) * 2 + z
                return pl.ds(pl.multiple_of(col + place * cols, 128), cols)

            pieces.append((moved(here), strip))
            moves = []
            for step, dz in PLANE:
                piece = parts.at[here, strip(step, lax.rem(me.z + dz, 2))]
                moves.append(links.send(piece, slot.at[step * 2 + dz - 1], to(step, dz)))
            yield
            for made in moves:
                made.wait_recv()
            mine = strip(0, me.z)
            add_rows(target, parts, here, mine, [slot.at[index] for index in range(7)], add)
            continue
        rows = rows // 4

        def chunk(step, row=row, rows=rows, spot=spot):
            return pl.ds(pl.multiple_of(row + lax.rem(spot + step, 4) * rows, 8), rows)

        pieces.append((chunk, across))
        if kind == "ring":
            low = pl.ds(col, cols // 2)
            high = pl.ds(col + cols // 2, cols // 2)
            first, second = pl.ds(0, cols // 2), pl.ds(cols // 2, cols // 2)
            side_up, side_down, main_up, main_down = slot
            far_up = links.send(parts.at[chunk(2), low], side_up, to(1))
            far_down = links.send(parts.at[chunk(2), high], side_down, to(3))
            near = [
                links.send(parts.at[chunk(1), high], main_up.at[:, second], to(1)),
                links.send(parts.at[chunk(3), low], main_down.at[:, first], to(3)),
            ]
            yield
            far_up.wait_recv()
            add_rows(parts, parts, chunk(1), low, [side_up])
            near.append(links.send(parts.at[chunk(1), low], main_up.at[:, first], to(1)))
            far_down.wait_recv()
            add_rows(parts, parts, chunk(3), high, [side_down])
            near.append(links.send(parts.at[chunk(3), high], main_down.at[:, second], to(3)))
            yield
            for made in near:
                made.wait_recv()
            add_rows(target, parts, chunk(0), across, [main_up, main_down], add)
            row = chunk(0).start
        else:
            moves = [
                links.send(parts.at[chunk(step), across], slot.at[step - 1], to(step))
                for step in (1, 3, 2)
            ]
            yield
            for made in moves:
                made.wait_recv()
            add_rows(target, parts, chunk(0), across, [slot.at[step] for step in range(3)], add)
            row = chunk(0).start
    for (kind, axis), (place, across) in zip(stages[::-1], pieces[::-1]):
        if kind == "pair":
            piece = whole.at[place, across]
            moves = [links.send(piece, piece, me.at(dz=1))]
            yield
        elif kind == "columns":
            _, to = ring(me, axis)
            piece = whole.at[place, across(0, me.z)]
            moves = [links.send(piece, piece, to(step, dz)) for step, dz in PLANE]
            yield
        elif kind == "direct":
            _, to = ring(me, axis)
            piece = whole.at[moved(place(0)), across]
            moves = [links.send(piece, piece, to(step)) for step in (1, 3, 2)]
            yield
        else:
            _, to = ring(me, axis)
            half = across.size // 2
            piece = whole.at[moved(place(0)), across]
            above = links.send(piece, piece, to(1))
            below = links.send(piece, piece, to(3))
            yield
            above.wait_recv()
            piece = whole.at[moved(place(3)), pl.ds(across.start, half)]
            moves = [links.send(piece, piece, to(1))]
            below.wait_recv()
            piece = whole.at[moved(place(1)), pl.ds(across.start + half, half)]
            moves.append(links.send(piece, piece, to(3)))
            yield
        for made in moves:
            made.wait_recv()
    copy = pltpu.make_async_copy(whole, result, done_sem)
    copy.start()
    yield
    copy.wait()


def head_sum(me, links, parts, whole, slots, result, done_sem, wide_last):
    count = parts.shape[0] // 8

    def rows(step, z):
        place = lax.rem(me.y + step, 4) * 2 + z
        return pl.ds(pl.multiple_of(place * count, count), count)

    moves = []
    for step, dz in PLANE:
        piece = parts.at[rows(step, lax.rem(me.z + dz, 2))]
        moves.append(links.send(piece, slots.at[step * 2 + dz - 1], me.at(dy=step, dz=dz)))
    yield
    for made in moves:
        made.wait_recv()
    mine = rows(0, me.z)
    value = parts[mine, :].astype(F32)
    for index in range(7):
        value = value + slots[index].astype(F32)
    whole[me.x, mine, :] = value.astype(BF16)
    for plane in (not wide_last, wide_last):
        if plane:
            piece = whole.at[:, mine] if wide_last else whole.at[me.x, mine]
            moves = [links.send(piece, piece, me.at(dy=step, dz=dz)) for step, dz in PLANE]
        else:
            piece = whole.at[me.x, mine] if wide_last else whole.at[me.x]
            moves = [links.send(piece, piece, me.at(dx=step)) for step in (1, 3, 2)]
        yield
        for made in moves:
            made.wait_recv()
    copy = pltpu.make_async_copy(whole, result, done_sem)
    copy.start()
    yield
    copy.wait()


PLANE = [(1, 0), (3, 0), (0, 1), (1, 1), (3, 1), (2, 0), (2, 1)]


def vector_sum(me, links, values, plane, line, total):
    own = me.group
    plane[own] = values[...]
    here = plane.at[own]
    moves = [links.send(here, here, me.at(dy=step, dz=dz)) for step, dz in PLANE]
    yield
    for made in moves:
        made.wait_recv()
    value = plane[0]
    for slot in range(1, 8):
        value = value + plane[slot]
    line[me.x] = value
    here = line.at[me.x]
    moves = [links.send(here, here, me.at(dx=step)) for step in (1, 3, 2)]
    yield
    for made in moves:
        made.wait_recv()
    total[...] = line[0] + line[1] + line[2] + line[3]


def x_share(me, links, slots):
    half = pl.ds(pl.multiple_of(me.core * 128, 128), 128)
    piece = slots.at[me.x, half]
    return [links.send(piece, piece, me.at(dx=step)) for step in (1, 3, 2)]


def core_share(me, links, slots, moves):
    half = pl.ds(pl.multiple_of(me.core * 128, 128), 128)
    passed = []
    for step, made in zip((3, 1, 2), moves):
        made.wait_recv()
        piece = slots.at[lax.rem(me.x + step, 4), half]
        passed.append(links.send(piece, piece, me.at(dcore=1)))
    return passed


PLAN = {
    "norm crossed": ("up", "first",),
    "norm back": ("up",),
    "heads sent": ("o",),
    "query one": ("up",),
    "query two": ("down",),
    "query three": ("up", "o",),
    "query four": ("up", "down",),
    "far wait": ("o", "up", "down",),
    "key one": ("down",),
    "vectors": ("o",),
    "key two": ("first", "vectors",),
    "key three": ("up",),
    "key four": ("down", "vectors", "first",),
    "head sums": ("kv", "q",),
    "low wait": ("down", "kv", "up",),
    "low back": ("q", "kv", "o", "o",),
    "last vectors": ("last",),
    "input ready": ("vectors", "q", "last", "kv", "kv", "up", "up",),
    "end": ("q", "down", "down", "last", "q",),
}


def share(me, links, slots):
    moves = x_share(me, links, slots)
    yield
    passed = core_share(me, links, slots, moves)
    yield
    for made in passed:
        made.wait_recv()


class Jobs:
    def __init__(self):
        self.live = {}

    def add(self, name, job):
        self.live[name] = job

    def step(self, name):
        if name in self.live and next(self.live[name], "done") == "done":
            del self.live[name]

    def drain(self, name):
        while name in self.live:
            self.step(name)

    def at(self, place):
        for name in PLAN.get(place, ()):
            self.step(name)

    def finish(self):
        while self.live:
            for name in list(self.live):
                self.step(name)


def list_mates(image_ref, next_of, mates, own):
    last = [jnp.int32(-1)] * 3
    for block in range(31, -1, -1):
        image = image_ref[block]
        next_of[block] = jnp.where(image == 0, last[0], jnp.where(image == 1, last[1], last[2]))
        last = [jnp.where(image == index, block, last[index]) for index in range(3)]
    for line in range(4):
        image = image_ref[line * 8 + own]
        first = jnp.where(image == 0, last[0], jnp.where(image == 1, last[1], last[2]))

        def list_one(index, block, line=line):
            known = jnp.maximum(block, 0)
            place = lax.rem(known, 8) * 4 + lax.div(known, 8)
            mates[line * 16 + index] = jnp.where(block < 0, -1, place)
            return jnp.where(block < 0, -1, next_of[known])

        lax.fori_loop(0, 16, list_one, first)


UP_STAGES = [("ring", "y"), ("direct", "x"), ("pair", None)]
DOWN_STAGES = [("summed", "x"), ("direct", "y"), ("pair", None)]
O_STAGES = [("direct", "x"), ("columns", "y")]


def layer_kernel(
    x_hbm, cot_hbm, gain_one_ref, shift_one_ref, weight_hbm, attend_bias_ref, output_hbm,
    output_bias_ref, gain_two_ref, shift_two_ref, up_hbm, up_bias_ref, down_hbm, down_bias_ref,
    image_ref,
    result_out, input_out, vector_out, last_out, up_out, down_out, kv_out, q_out, o_out,
    x_ref, cot_ref, weight_ref, up_ref, down_ref,
    first_all, down_all, activated_all, kv, query_pair, kv_send, query_send, query_own, top, total, mixed,
    head_send, head_recv, attended, output_all, next_of, mates,
    hidden, xhat_two, inverse_two, second_low, activated, pre_grad,
    branch_low, norm_parts, unit_parts, low_parts,
    grad_send, grad_pair, stats_all, grad_own, rows_all, query_grad_all,
    qg_own, qg_send, qg_recv, kvg_send, kvg_recv, stacked, flat,
    vector, plane_one, line_one, last, plane_two, line_two,
    job_up, job_down, job_kv, job_q, job_o,
    send_sem, recv_sem, load_sem, done_sem,
):
    me = Place()
    links = Links(send_sem, recv_sem)
    at = me.high * 2 + me.core
    loads = []
    for source, target in (
        (x_hbm, x_ref), (weight_hbm, weight_ref), (output_hbm, output_all.at[at]),
        (cot_hbm, cot_ref), (up_hbm, up_ref), (down_hbm, down_ref),
    ):
        load = pltpu.make_async_copy(source, target, load_sem.at[len(loads)])
        load.start()
        loads.append(load)
    wait_all = greet(all_partners(me))
    own = me.group
    loads[0].wait()
    normed, _ = row_norm(x_ref[...])
    first_low = (normed * gain_one_ref[...] + shift_one_ref[...]).astype(BF16)
    first_all[me.x] = first_low
    loads[1].wait()
    keys = dot_nn(first_low, weight_ref[1])
    values = dot_nn(first_low, weight_ref[2]) + attend_bias_ref[1:2, :]
    for head in range(4):
        part = slice(head * HEAD_DIM, (head + 1) * HEAD_DIM)
        kv_send[head] = jnp.concatenate([keys[:, part], values[:, part]], axis=1).astype(BF16)
    wait_all()
    kv_moves, query_moves = [], []
    for step in (1, 3, 2):
        head = lax.rem(me.x + step, 4)
        kv_moves.append(links.send(kv_send.at[head], kv.at[own * 4 + me.x], me.at(dx=step)))
    loads[2].wait()
    quarter = pl.ds(pl.multiple_of(me.x * 64, 64), 64)
    piece = output_all.at[at, quarter]
    output_high = links.send(piece, piece, me.at(dhigh=1))
    queries = dot_nn(first_low, weight_ref[0]) + attend_bias_ref[0:1, :]
    pack_heads(queries.astype(BF16).astype(F32) * (HEAD_DIM**-0.5), query_send)
    for step in (1, 3, 2):
        head = lax.rem(me.x + step, 4)
        query_moves.append(
            links.send(query_send.at[head], query_pair.at[own * 4 + me.x], me.at(dx=step))
        )
    kv[own * 4 + me.x] = kv_send[me.x]
    query_pair[own * 4 + me.x] = query_send[me.x]
    output_core = links.send(output_all.at[at], output_all.at[at], me.at(dcore=1))
    loads[3].wait()
    down_all[me.x] = cot_ref[...].astype(BF16)
    down_moves = x_share(me, links, down_all)
    for made in kv_moves:
        made.wait_recv()
    gather = Gather(me, links, kv)
    gather.begin()
    top[...] = jnp.full(top.shape, LOWEST, F32)
    total[...] = jnp.zeros(total.shape, F32)
    mixed[...] = jnp.zeros(mixed.shape, F32)
    list_mates(image_ref, next_of, mates, own)
    for made in query_moves:
        made.wait_recv()
    for block in range(4):
        pair = query_pair[own * 4 + block].astype(F32)
        both = jnp.concatenate([pair, pltpu.roll(pair, 64, 1)], axis=0)
        query_own[block] = jnp.where(lanes_below(both.shape), both, 0.0).astype(BF16)

    def attend(slot):
        keys = [kv[slot * 4 + part] for part in range(4)]
        images = [image_ref[part * 8 + slot] for part in range(4)]
        scores = [[dot_nt(query_own[block], key) for key in keys] for block in range(4)]
        joined = jnp.concatenate(keys, axis=0)
        state = []
        for block in range(4):
            mine = image_ref[block * 8 + own]
            highest, shut = None, []
            for part in range(4):
                same = images[part] == mine
                shut.append(jnp.where(same, -3e38, HIGHEST))
                score = scores[block][part]
                peak = jnp.maximum(score[:, :128], score[:, 128:])
                peak = jnp.minimum(peak, jnp.where(same, 3e38, LOWEST))
                highest = peak if highest is None else jnp.maximum(highest, peak)
            before = top[block]
            now = jnp.maximum(before, spread(jnp.max(highest, axis=1, keepdims=True)))
            top[block] = now
            state.append((now, jnp.exp(before - now), shut))
        for block, (now, fade, shut) in enumerate(state):
            sums = total[block] * fade
            probs = []
            for part in range(4):
                level = jnp.maximum(now, shut[part])
                prob = jnp.exp(scores[block][part] - wide(level))
                sums = sums + prob[:, :128] + prob[:, 128:]
                probs.append(prob.astype(BF16))
            total[block] = sums
            mixed[block] = mixed[block] * fade + dot_nn(jnp.concatenate(probs, axis=1), joined)

    def attend_near(z):
        @pl.loop(0, 2)
        def _(side):
            attend(gather.slot(3 - 2 * side, z))

    across = (1 - me.high) * 2 + me.core
    output_high.wait_recv()
    piece = output_all.at[across, quarter]
    output_moves = [links.send(piece, piece, me.at(dx=step)) for step in (1, 3, 2)]
    attend(own)
    gather.pass_z()
    attend(gather.slot(0, gather.other))
    gather.pass_own()
    attend_near(me.z)
    gather.pass_other()
    gather.end_own()
    attend(gather.slot(2, me.z))
    gather.end_near()
    attend_near(gather.other)
    gather.end_other()
    query_gather = Gather(me, links, query_pair)
    query_gather.begin()
    attend(gather.slot(2, gather.other))
    for block in range(4):
        sums = spread(jnp.sum(total[block], axis=1, keepdims=True))
        out = mixed[block] / sums
        mixed[block] = out
        top[block] = top[block] + jnp.log(sums)
        back = pltpu.roll(out[:128, :], 64, 1)
        head_send[block] = jnp.where(lanes_below(back.shape), back, out[128:, :]).astype(BF16)
    head_moves, high_moves = [], []
    for step in (1, 3, 2):
        piece = head_send.at[lax.rem(me.x + step, 4)]
        head_moves.append(links.send(piece, head_recv.at[me.x], me.at(dx=step)))
        high_moves.append(links.send(piece, head_recv.at[me.x + 4], me.at(dx=step, dhigh=1)))
    high_moves.append(
        links.send(head_send.at[me.x], head_recv.at[me.x + 4], me.at(dhigh=1))
    )
    head_recv[me.x] = head_send[me.x]
    for made in output_moves:
        made.wait_recv()
    output_pass = links.send(output_all.at[across], output_all.at[across], me.at(dcore=1))
    down_pass = core_share(me, links, down_all, down_moves)
    for block in range(4):
        stats_all[own, block : block + 1, :] = top[block].T[0:1, :]
    for made in head_moves:
        made.wait_recv()
    attended[at] = unpack_heads(head_recv.at[0:4])
    attended_core = links.send(attended.at[at], attended.at[at], me.at(dcore=1))
    query_gather.pass_z()
    for made in high_moves:
        made.wait_recv()
    attended[across] = unpack_heads(head_recv.at[4:8])
    attended_pass = links.send(attended.at[across], attended.at[across], me.at(dcore=1))
    query_gather.pass_own()
    output_core.wait_recv()
    output_pass.wait_recv()
    query_gather.pass_other()
    attended_core.wait_recv()
    attended_pass.wait_recv()

    @pl.loop(0, 4)
    def _(step):
        cols = cols_of(step)
        value = x_ref[:, cols] + output_bias_ref[:, cols]
        for part in range(4):
            value = value + dot_nn(attended[part], output_all[part, :, cols])
        hidden[:, cols] = value

    normed, inverse = row_norm(hidden[...])
    xhat_two[...] = normed
    inverse_two[...] = spread(inverse)
    second_low[...] = (normed * gain_two_ref[...] + shift_two_ref[...]).astype(BF16)
    loads[4].wait()
    loads[5].wait()

    @pl.loop(0, 4)
    def _(step):
        cols = cols_of(step)
        pre = dot_nn(second_low[...], up_ref[:, cols]) + up_bias_ref[:, cols]
        back = dot_nt(down_all[me.x], down_ref[cols, :])
        chance = 0.5 + 0.5 * lax.erf(pre * (0.5**0.5))
        density = jnp.exp(-0.5 * pre * pre) * 0.3989422804014327
        activated[:, cols] = (pre * chance).astype(BF16)
        low = (back * (chance + pre * density)).astype(BF16)
        pre_grad[:, cols] = low
        vector[4:5, cols] = jnp.sum(low.astype(F32), axis=0, keepdims=True)

    act_moves = []
    for step in (1, 3, 2):
        piece = activated.at[:, cols_of(lax.rem(me.x + step, 4))]
        act_moves.append(links.send(piece, activated_all.at[me.x], me.at(dx=step)))
    norm_sum = ModelSum(me, links, *norm_parts)
    norm_sum.begin(lambda cols: dot_nt(pre_grad[...], up_ref[cols, :]))

    for side in range(2):

        @pl.loop(2 * side, 2 * side + 2)
        def _(step):
            cols = cols_of(step)
            job_up[0][cols, :] = dot_tn(second_low[:, cols], pre_grad[...]).astype(BF16)

        norm_sum.cross(side)

    jobs = Jobs()
    jobs.add("first", share(me, links, first_all))
    jobs.add("up", weight_sum(me, links, UP_STAGES, *job_up, up_out, done_sem.at[0]))
    query_gather.end_near()
    query_gather.end_own()
    query_gather.end_other()
    jobs.at("norm crossed")
    unit_sum = ModelSum(me, links, *unit_parts)
    unit_sum.begin(lambda cols: dot_nn(activated[...], down_ref[:, cols]))
    vector[3:4, :] = jnp.sum(down_all[me.x].astype(F32), axis=0, keepdims=True)
    activated_all[me.x] = activated[:, cols_of(me.x)]
    for made in down_pass + act_moves:
        made.wait_recv()

    @pl.loop(0, 4)
    def _(step):
        cols = cols_of(step)
        value = dot_tn(activated_all[0], down_all[0, :, cols])
        for spot in range(1, 4):
            value = value + dot_tn(activated_all[spot], down_all[spot, :, cols])
        job_down[0][:, cols] = value.astype(BF16)

    jobs.add("down", weight_sum(me, links, DOWN_STAGES, *job_down, down_out, done_sem.at[1]))
    jobs.at("partner wait")
    norm_sum.back()
    jobs.at("norm back")
    norm_sum.end()
    grad = norm_sum.full[...].astype(F32)
    xhat = xhat_two[...]
    vector[0:1, :] = jnp.sum(grad * xhat, axis=0, keepdims=True)
    vector[1:2, :] = jnp.sum(grad, axis=0, keepdims=True)
    scaled = grad * gain_two_ref[...]
    hidden_grad = cot_ref[...] + (
        scaled
        - jnp.mean(scaled, axis=-1, keepdims=True)
        - xhat * jnp.mean(scaled * xhat, axis=-1, keepdims=True)
    ) * inverse_two[:, 0:1]
    cot_ref[...] = hidden_grad
    low = hidden_grad.astype(BF16)
    branch_low[...] = low
    vector[2:3, :] = jnp.sum(low.astype(F32), axis=0, keepdims=True)
    pack_heads(dot_nt(branch_low[...], output_all[at]).astype(BF16).astype(F32), grad_send)
    moves = []
    for step in (1, 3, 2):
        head = lax.rem(me.x + step, 4)
        moves.append(links.send(grad_send.at[head], grad_pair.at[own * 4 + me.x], me.at(dx=step)))
    grad_pair[own * 4 + me.x] = grad_send[me.x]

    @pl.loop(0, 4)
    def _(step):
        cols = cols_of(step)
        job_o[0][:, cols] = dot_tn(attended[at], branch_low[:, cols]).astype(BF16)

    jobs.add("o", weight_sum(me, links, O_STAGES, *job_o, o_out, done_sem.at[2]))
    jobs.at("heads sent")
    for made in moves:
        made.wait_recv()
    gather = Gather(me, links, grad_pair)
    gather.begin()

    @pl.loop(0, 4)
    def _(block):
        pair = grad_pair[own * 4 + block].astype(F32)
        both = jnp.concatenate([pltpu.roll(pair, 64, 1), pair], axis=0)
        both = jnp.where(lanes_below(both.shape), 0.0, both)
        grad_own[block] = both.astype(BF16)
        delta = spread(jnp.sum(both * mixed[block], axis=1, keepdims=True))
        total[block] = delta
        stats_all[own, pl.ds(block + 4, 1), :] = delta.T[0:1, :]

    here = stats_all.at[own]
    stats_moves = [links.send(here, here, me.at(dy=step, dz=dz)) for step, dz in PLANE]

    def query_pass(block):
        query, grad_out = query_own[block], grad_own[block]
        level, delta = top[block], wide(total[block])

        def some(step, acc):
            keys, changes = [], []
            for part in range(8):
                place = mates[block * 16 + step * 8 + part]
                key = kv[jnp.maximum(place, 0)]
                shut = jnp.where(place < 0, HIGHEST, -3e38)
                prob = jnp.exp(dot_nt(query, key) - wide(jnp.maximum(level, shut)))
                changes.append((prob * (dot_nt(grad_out, key) - delta)).astype(BF16))
                keys.append(key)
            return acc + dot_nn(jnp.concatenate(changes, axis=1), jnp.concatenate(keys, axis=0))

        acc = lax.fori_loop(0, 2, some, jnp.zeros((256, 128), F32)) * (HEAD_DIM**-0.5)
        qg_own[block] = acc.astype(BF16)
        qg_send[block] = pack_rows(acc).astype(BF16)

    query_moves = []

    def send_query(step):
        block = lax.rem(me.x + step, 4)
        query_pass(block)
        if step:
            query_moves.append(links.send(qg_send.at[block], qg_recv.at[me.x], me.at(dx=step)))
        else:
            qg_recv[me.x] = qg_send[me.x]

    def pair_up(slot):
        @pl.loop(0, 4)
        def _(block):
            spot = slot * 4 + block
            pair = query_pair[spot].astype(F32)
            other = grad_pair[spot].astype(F32)
            keep = lanes_below(pair.shape)
            upper = jnp.where(keep, pair, pltpu.roll(other, 64, 1))
            lower = jnp.where(keep, pltpu.roll(pair, 64, 1), other)
            query_grad_all[spot] = jnp.concatenate([upper, lower], axis=0).astype(BF16)
            rows_all[spot, 0:1, :] = stats_all[slot, pl.ds(block, 1), :]
            rows_all[spot, 1:2, :] = stats_all[slot, pl.ds(block + 4, 1), :]

    jobs.at("gather begun")
    send_query(2)
    jobs.at("query one")
    send_query(1)
    gather.pass_z()
    gather.pass_own()
    jobs.at("query two")
    for made in stats_moves:
        made.wait_recv()
    pair_up(own)
    pair_up(gather.slot(0, gather.other))
    send_query(3)
    gather.pass_other()
    gather.end_own()
    jobs.at("query three")
    pair_up(gather.slot(1, me.z))
    pair_up(gather.slot(3, me.z))
    send_query(0)
    jobs.at("query four")
    gather.end_near()
    pair_up(gather.slot(2, me.z))
    pair_up(gather.slot(1, gather.other))
    pair_up(gather.slot(3, gather.other))
    jobs.at("far wait")
    gather.end_other()
    pair_up(gather.slot(2, gather.other))
    unit_sum.cross(0)
    unit_sum.cross(1)
    jobs.at("gathered")

    def key_pass(block):
        both = kv[own * 4 + block].astype(F32)
        keep = lanes_below(both.shape)
        key = jnp.where(keep, both, 0.0).astype(BF16)
        value = jnp.where(keep, 0.0, both).astype(BF16)

        def some(step, accs):
            pairs, probs, changes = [], [], []
            for part in range(8):
                place = mates[block * 16 + step * 8 + part]
                spot = jnp.maximum(place, 0)
                shut = jnp.where(place < 0, HIGHEST, -3e38)
                pair, lines = query_grad_all[spot], rows_all[spot]
                prob = jnp.exp(dot_nt(key, pair) - jnp.maximum(lines[0:1, :], shut))
                probs.append(prob.astype(BF16))
                changes.append((prob * (dot_nt(value, pair) - lines[1:2, :])).astype(BF16))
                pairs.append(pair)
            joined = jnp.concatenate(pairs, axis=0)
            return (
                accs[0] + dot_nn(jnp.concatenate(changes, axis=1), joined),
                accs[1] + dot_nn(jnp.concatenate(probs, axis=1), joined),
            )

        zero = jnp.zeros((256, 128), F32)
        of_key, of_value = lax.fori_loop(0, 2, some, (zero, zero))
        kvg_send[block] = jnp.where(keep, of_key, of_value).astype(BF16)

    key_moves = []

    def send_key(step):
        block = lax.rem(me.x + step, 4)
        key_pass(block)
        if step:
            key_moves.append(links.send(kvg_send.at[block], kvg_recv.at[me.x], me.at(dx=step)))
        else:
            kvg_recv[me.x] = kvg_send[me.x]

    send_key(2)
    jobs.at("key one")
    vector[5:8, :] = jnp.zeros((3, 1024), F32)
    jobs.add("vectors", vector_sum(me, links, vector, plane_one, line_one, vector_out))
    jobs.at("vectors")
    send_key(1)
    jobs.at("key two")
    for made in query_moves:
        made.wait_recv()
    stacked[:, 0:256] = unpack_heads(qg_recv)
    send_key(3)
    jobs.at("key three")
    send_key(0)
    unit_sum.back()
    jobs.at("key four")

    jobs.drain("first")

    def own_grads(block):
        return jnp.concatenate([kvg_send[block], qg_own[block]], axis=1)

    @pl.loop(0, 4)
    def _(step):
        cols = cols_of(step)
        value = dot_tn(first_all[0, :, cols], own_grads(0))
        for spot in range(1, 4):
            value = value + dot_tn(first_all[spot, :, cols], own_grads(spot))
        job_kv[0][cols, :] = value[:, :128].astype(BF16)
        flat[cols, :] = value[:, 128:]

    job_q[0][...] = jnp.where(
        lanes_below((512, 128)), flat[0:512, :], pltpu.roll(flat[512:1024, :], 64, 1)
    ).astype(BF16)
    jobs.add("kv", head_sum(me, links, *job_kv, kv_out, done_sem.at[3], False))
    jobs.add("q", head_sum(me, links, *job_q, q_out, done_sem.at[4], True))
    jobs.at("head sums")
    for made in key_moves:
        made.wait_recv()

    back = [kvg_recv[head].astype(F32) for head in range(4)]
    stacked[:, 256:512] = jnp.concatenate([value[:, :64] for value in back], axis=1).astype(BF16)
    stacked[:, 512:768] = jnp.concatenate([value[:, 64:] for value in back], axis=1).astype(BF16)
    low_sum = ModelSum(me, links, *low_parts)
    low_sum.begin(
        lambda cols: dot_nt(stacked[:, 0:256], weight_ref[0, cols, :])
        + dot_nt(stacked[:, 256:512], weight_ref[1, cols, :])
        + dot_nt(stacked[:, 512:768], weight_ref[2, cols, :])
    )
    low_sum.cross(0)
    last[8:9, :] = jnp.sum(stacked[:, 0:256].astype(F32), axis=0, keepdims=True)
    last[9:10, :] = jnp.sum(stacked[:, 512:768].astype(F32), axis=0, keepdims=True)
    last[10:16, :] = jnp.zeros((6, 256), F32)
    low_sum.cross(1)
    jobs.at("low crossed")
    xhat, inverse = row_norm(x_ref[...])
    jobs.at("low wait")
    low_sum.back()
    jobs.at("low back")
    low_sum.end()
    grad = low_sum.full[...].astype(F32)
    gain_grad = jnp.sum(grad * xhat, axis=0, keepdims=True)
    shift_grad = jnp.sum(grad, axis=0, keepdims=True)
    for part in range(4):
        cols = slice(part * 256, (part + 1) * 256)
        last[part : part + 1, :] = gain_grad[:, cols]
        last[part + 4 : part + 5, :] = shift_grad[:, cols]
    jobs.add("last", vector_sum(me, links, last, plane_two, line_two, last_out))
    jobs.at("last vectors")
    scaled = grad * gain_one_ref[...]
    cot_ref[...] = cot_ref[...] + (
        scaled
        - jnp.mean(scaled, axis=-1, keepdims=True)
        - xhat * jnp.mean(scaled * xhat, axis=-1, keepdims=True)
    ) * inverse
    input_done = pltpu.make_async_copy(cot_ref, input_out, done_sem.at[6])
    input_done.start()
    unit_sum.end()
    hidden[...] = hidden[...] + unit_sum.full[...].astype(F32) + down_bias_ref[...]
    result_done = pltpu.make_async_copy(hidden, result_out, done_sem.at[7])
    result_done.start()
    jobs.at("input ready")
    jobs.at("end")
    jobs.finish()
    input_done.wait()
    result_done.wait()
    links.finish()


def job_scratch(height, width, stages):
    slots = []
    rows, cols = height, width
    for kind, _ in stages:
        if kind == "ring":
            rows = rows // 4
            side, main = pltpu.VMEM((rows, cols // 2), BF16), pltpu.VMEM((rows, cols), BF16)
            slots.append([side, side, main, main])
        elif kind == "direct":
            rows = rows // 4
            slots.append(pltpu.VMEM((3, rows, cols), BF16))
        elif kind == "summed":
            slots.append(pltpu.SMEM((1,), jnp.int32))
        elif kind == "columns":
            cols = cols // 8
            slots.append(pltpu.VMEM((7, rows, cols), BF16))
        else:
            cols = cols // 2
            slots.append(pltpu.VMEM((rows, cols), BF16))
    full = height * 4 if stages[0][0] == "summed" else height
    return [pltpu.VMEM((height, width), BF16), pltpu.VMEM((full, width), BF16), slots]


def head_scratch(rows):
    return [
        pltpu.VMEM((rows, 128), BF16),
        pltpu.VMEM((4, rows, 128), BF16),
        pltpu.VMEM((7, rows // 8, 128), BF16),
    ]


def sum_scratch():
    half = pltpu.VMEM((128, 1024), BF16)
    whole = pltpu.VMEM((256, 1024), BF16)
    return [whole, half, half, half, whole]


def layer(*args):
    vmem = pl.BlockSpec(memory_space=pltpu.VMEM)
    smem = pl.BlockSpec(memory_space=pltpu.SMEM)
    hbm = pl.BlockSpec(memory_space=pl.ANY)
    low_rows = pltpu.VMEM((256, 1024), BF16)
    wide_rows = pltpu.VMEM((256, 1024), F32)
    return pl.pallas_call(
        layer_kernel,
        out_shape=[
            jax.ShapeDtypeStruct((256, 1024), F32),
            jax.ShapeDtypeStruct((256, 1024), F32),
            jax.ShapeDtypeStruct((8, 1024), F32),
            jax.ShapeDtypeStruct((16, 256), F32),
            jax.ShapeDtypeStruct((1024, 1024), BF16),
            jax.ShapeDtypeStruct((1024, 1024), BF16),
            jax.ShapeDtypeStruct((4, 1024, 128), BF16),
            jax.ShapeDtypeStruct((4, 512, 128), BF16),
            jax.ShapeDtypeStruct((256, 1024), BF16),
        ],
        in_specs=[hbm, hbm, vmem, vmem, hbm, vmem, hbm, vmem, vmem, vmem, hbm, vmem, hbm, vmem, smem],
        out_specs=[hbm] * 2 + [vmem] * 2 + [hbm] * 5,
        scratch_shapes=[
            wide_rows, wide_rows,
            pltpu.VMEM((3, 1024, 256), BF16),
            pltpu.VMEM((1024, 1024), BF16), pltpu.VMEM((1024, 1024), BF16),
            pltpu.VMEM((4, 256, 1024), BF16),
            pltpu.VMEM((4, 256, 1024), BF16),
            pltpu.VMEM((4, 256, 256), BF16),
            pltpu.VMEM((32, 256, 128), BF16),
            pltpu.VMEM((32, 128, 128), BF16),
            pltpu.VMEM((4, 256, 128), BF16),
            pltpu.VMEM((4, 128, 128), BF16),
            pltpu.VMEM((4, 256, 128), BF16),
            pltpu.VMEM((4, 256, 128), F32),
            pltpu.VMEM((4, 256, 128), F32),
            pltpu.VMEM((4, 256, 128), F32),
            pltpu.VMEM((4, 128, 128), BF16),
            pltpu.VMEM((8, 128, 128), BF16),
            pltpu.VMEM((4, 256, 256), BF16),
            pltpu.VMEM((4, 256, 1024), BF16),
            pltpu.SMEM((32,), jnp.int32),
            pltpu.SMEM((64,), jnp.int32),
            wide_rows, wide_rows, pltpu.VMEM((256, 128), F32),
            low_rows, low_rows, low_rows, low_rows,
            sum_scratch(), sum_scratch(), sum_scratch(),
            pltpu.VMEM((4, 128, 128), BF16),
            pltpu.VMEM((32, 128, 128), BF16),
            pltpu.VMEM((8, 8, 256), F32),
            pltpu.VMEM((4, 256, 128), BF16),
            pltpu.VMEM((32, 8, 256), F32),
            pltpu.VMEM((32, 256, 128), BF16),
            pltpu.VMEM((4, 256, 128), BF16),
            pltpu.VMEM((4, 128, 128), BF16),
            pltpu.VMEM((4, 128, 128), BF16),
            pltpu.VMEM((4, 256, 128), BF16),
            pltpu.VMEM((4, 256, 128), BF16),
            pltpu.VMEM((256, 768), BF16),
            pltpu.VMEM((1024, 128), F32),
            pltpu.VMEM((8, 1024), F32), pltpu.VMEM((8, 8, 1024), F32), pltpu.VMEM((4, 8, 1024), F32),
            pltpu.VMEM((16, 256), F32), pltpu.VMEM((8, 16, 256), F32), pltpu.VMEM((4, 16, 256), F32),
            job_scratch(1024, 1024, UP_STAGES),
            job_scratch(256, 1024, DOWN_STAGES),
            head_scratch(1024),
            head_scratch(512),
            job_scratch(256, 1024, O_STAGES),
            pltpu.SemaphoreType.DMA((240,)),
            pltpu.SemaphoreType.DMA((240,)),
            pltpu.SemaphoreType.DMA((6,)),
            pltpu.SemaphoreType.DMA((8,)),
        ],
        compiler_params=pltpu.CompilerParams(
            collective_id=0, has_side_effects=True, vmem_limit_bytes=VMEM_BYTES
        ),
    )(*args)


def widen_kernel(
    up, down, kv, q, o, result, input_grad, vector, last,
    up_out, down_out, qkv_out, o_out, result_out, input_out,
    first_gain, first_shift, bias, output_bias, second_gain, second_shift, up_bias, down_bias,
):
    up_out[...] = up[...].astype(F32)
    down_out[...] = down[...].astype(F32)
    pairs = [kv[head].astype(F32) for head in range(4)]
    qkv_out[1] = jnp.concatenate([pair[:, :HEAD_DIM] for pair in pairs], axis=1)
    qkv_out[2] = jnp.concatenate([pair[:, HEAD_DIM:] for pair in pairs], axis=1)
    pairs = [q[head].astype(F32) for head in range(4)]
    upper = jnp.concatenate([pair[:, :HEAD_DIM] for pair in pairs], axis=1)
    lower = jnp.concatenate([pair[:, HEAD_DIM:] for pair in pairs], axis=1)
    qkv_out[0] = jnp.where(pl.program_id(0) < pl.num_programs(0) // 2, upper, lower)
    o_out[...] = o[...].astype(F32)
    result_out[...] = result[...]
    input_out[...] = input_grad[...]

    @pl.when(pl.program_id(0) == 0)
    def _():
        first_gain[...] = jnp.concatenate([last[row : row + 1, :] for row in range(4)], axis=1)
        first_shift[...] = jnp.concatenate([last[row : row + 1, :] for row in range(4, 8)], axis=1)
        bias[...] = last[8:10, :]
        for target, row in (
            (second_gain, 0), (second_shift, 1), (output_bias, 2), (down_bias, 3), (up_bias, 4),
        ):
            target[...] = vector[row : row + 1, :]


def widen(up, down, kv, q, o, result, input_grad, vector, last):
    steps = 8
    tall = pl.BlockSpec((1024 // steps, 1024), lambda step: (step, 0))
    short = pl.BlockSpec((256 // steps, 1024), lambda step: (step, 0))
    three = pl.BlockSpec((3, 1024 // steps, 256), lambda step: (0, step, 0))
    line = pl.BlockSpec((1, 1024), lambda step: (0, 0))

    def whole(shape):
        return pl.BlockSpec(shape, lambda step: (0, 0))

    row = jax.ShapeDtypeStruct((1, 1024), F32)
    return pl.pallas_call(
        widen_kernel,
        grid=(steps,),
        out_shape=[
            jax.ShapeDtypeStruct((1024, 1024), F32),
            jax.ShapeDtypeStruct((1024, 1024), F32),
            jax.ShapeDtypeStruct((3, 1024, 256), F32),
            jax.ShapeDtypeStruct((256, 1024), F32),
            jax.ShapeDtypeStruct((256, 1024), F32),
            jax.ShapeDtypeStruct((256, 1024), F32),
            row, row, jax.ShapeDtypeStruct((2, 256), F32), row, row, row, row, row,
        ],
        in_specs=[
            tall, tall,
            pl.BlockSpec((4, 1024 // steps, 128), lambda step: (0, step, 0)),
            pl.BlockSpec((4, 1024 // steps, 128), lambda step: (0, lax.rem(step, steps // 2), 0)),
            short, short, short, whole((8, 1024)), whole((16, 256)),
        ],
        out_specs=[
            tall, tall, three, short, short, short,
            line, line, whole((2, 256)), line, line, line, line, line,
        ],
        compiler_params=pltpu.CompilerParams(vmem_limit_bytes=VMEM_BYTES),
    )(up, down, kv, q, o, result, input_grad, vector, last)


def per_device(
    inputs,
    first_gain,
    first_shift,
    attend_weight,
    attend_bias,
    output_weight,
    output_bias,
    second_gain,
    second_shift,
    up_weight,
    up_bias,
    down_weight,
    down_bias,
    image_of,
    cotangent,
):
    result, input_grad, vector, last, up, down, kv, q, o = layer(
        inputs, cotangent, first_gain[None], first_shift[None], attend_weight, attend_bias,
        output_weight, output_bias[None], second_gain[None], second_shift[None],
        up_weight, up_bias[None], down_weight, down_bias[None], image_of,
    )
    (
        up, down, qkv, o, result, input_grad, first_gain_grad, first_shift_grad, bias_grad,
        output_bias_grad, second_gain_grad, second_shift_grad, up_bias_grad, down_bias_grad,
    ) = widen(up, down, kv, q, o, result, input_grad, vector, last)
    return (
        result, input_grad, first_gain_grad[0], first_shift_grad[0], qkv, bias_grad, o,
        output_bias_grad[0], second_gain_grad[0], second_shift_grad[0], up, up_bias_grad[0], down,
        down_bias_grad[0],
    )


def solution(mesh):
    in_specs = (
        P("dp", None), P(), P(), P(None, None, "mp"), P(None, "mp"), P("mp", None), P(), P(), P(),
        P(None, "mp"), P("mp"), P("mp", None), P(), P(), P("dp", None),
    )
    out_specs = (
        P("dp", None), P("dp", None), P(), P(), P(None, None, "mp"), P(None, "mp"), P("mp", None),
        P(), P(), P(), P(None, "mp"), P("mp"), P("mp", None), P(),
    )
    return jax.shard_map(
        per_device, mesh=mesh, in_specs=in_specs, out_specs=out_specs, check_vma=False
    )
```
